512 devices in a mesh: seq: 64 (over x, y, core), head: 8 (over z).
Axes of the slice: x: 4, y: 8, z: 8, core: 2. Of those that a mesh axis runs over, the one named last changes fastest.
Arguments:
- query_rows: bfloat16 [32768, 1024], P(('seq', 'head')), may hold values from -16 to 16
- key_rows: bfloat16 [32768, 1024], P(('seq', 'head')), may hold values from -16 to 16
- value_rows: bfloat16 [32768, 1024], P(('seq', 'head')), may hold values from -6 to 6
- out_grad: bfloat16 [32768, 1024], P(('seq', 'head')), may hold values from -6 to 6
- random_blocks: int32 [512, 2], P('seq'), may hold values from 0 to 511, as said below
- global_blocks: int32 [2], replicated, may hold values from 0 to 511
Outputs:
- attn_out: bfloat16 [32768, 1024], P(('seq', 'head'))
- q_grad: bfloat16 [32768, 1024], P(('seq', 'head'))
- k_grad: bfloat16 [32768, 1024], P(('seq', 'head'))
- v_grad: bfloat16 [32768, 1024], P(('seq', 'head'))
The draws below stay inside these ranges and needn't reach their ends.
Inputs may be any that keep to these rules, and one draw needn't show every extreme that they name: `random_blocks`: the 16 random blocks named by the query blocks of one device belong to 16 different devices along `seq`: at most one of them lies among any one device's 8 blocks.
All inputs are finite; a program needn't handle non-finite values.
Results may differ from the reference program's by a relative error of at most 0.011.
Values may be sent and summed in bfloat16 or wider, within the bound.
No kernel may reach another device: no remote copies, remote signals or barrier semaphores. Data moves between devices by JAX's collectives and lax.ppermute only.
A program may use at most 64 MiB of HBM per device.

```python
import jax
import jax.numpy as jnp
from jax import lax

HEADS = 16
HEAD_DIM = 64
BLOCK = 64
RANDOM = 2
GLOBALS = 2
BLK_DEV = 8
SEQLEN = 32768
NBLK = 512
CAP = 1
N_SEQ = 64


def draw_query_rows(key, part):
    noise = jax.random.normal(jax.random.fold_in(key, 11), (SEQLEN, HEADS, HEAD_DIM), jnp.float32)
    values_drawn = jnp.clip(noise, -6.0, 6.0)
    return jnp.clip(values_drawn, -16.0, 16.0).reshape(SEQLEN, HEADS * HEAD_DIM).astype(jnp.bfloat16)


def draw_key_rows(key, part):
    noise = jax.random.normal(jax.random.fold_in(key, 13), (SEQLEN, HEADS, HEAD_DIM), jnp.float32)
    values_drawn = jnp.clip(noise, -6.0, 6.0)
    return jnp.clip(values_drawn, -16.0, 16.0).reshape(SEQLEN, HEADS * HEAD_DIM).astype(jnp.bfloat16)


def draw_random_blocks(key, part):
    slot_total = N_SEQ * CAP
    per_device = RANDOM * BLK_DEV
    device_keys = jax.random.split(jax.random.fold_in(key, 3), N_SEQ)

    def one_device(device_key):
        order = jax.random.permutation(jax.random.fold_in(device_key, 1), slot_total)[:per_device]
        source = order // CAP
        within = jax.random.randint(jax.random.fold_in(device_key, 2), (per_device,), 0, BLK_DEV)
        return (source * BLK_DEV + within).astype(jnp.int32)
    return jax.vmap(one_device)(device_keys).reshape(NBLK, RANDOM).astype(jnp.int32)


def block_levels(key, shape, pieces, smallest, high):
    loudness, own = 1.0, jax.random.fold_in(key, 6)
    for dim, parts in pieces:
        steps = jnp.exp(jax.random.uniform(jax.random.fold_in(own, dim), (parts,), jnp.float32, smallest / len(pieces), high / len(pieces)))
        loudness = loudness * jnp.repeat(steps, shape[dim] // parts).reshape([-1 if axis == dim else 1 for axis in range(len(shape))])
    return loudness


def gaussian(key, dims, width, bound, pieces=(), kind=jnp.bfloat16):
    drawn = width * jax.random.normal(key, dims, jnp.float32)
    if pieces:
        drawn = drawn * block_levels(key, dims, pieces, -0.22, 0.18)
    return jnp.clip(drawn, -bound, bound).astype(kind)


def setup_inputs(seed: int = 0) -> dict:
    streams_of = jax.random.split(jax.random.key(seed), 7)
    query_rows = draw_query_rows(jax.random.fold_in(streams_of[6], 71), 0)
    key_rows = draw_key_rows(jax.random.fold_in(streams_of[6], 71), 0)
    value_rows = gaussian(streams_of[2], (SEQLEN, HEADS * HEAD_DIM), 1.0, 6.0, ((0, 512),))
    out_grad = gaussian(streams_of[3], (SEQLEN, HEADS * HEAD_DIM), 1.0, 6.0, ((0, 512),))
    random_blocks = draw_random_blocks(jax.random.fold_in(streams_of[6], 71), 0)
    global_blocks = jax.random.randint(streams_of[5], (GLOBALS,), 0, NBLK).astype(jnp.int32)
    return dict(query_rows=query_rows, key_rows=key_rows, value_rows=value_rows, out_grad=out_grad, random_blocks=random_blocks, global_blocks=global_blocks)


masked_score = -1e30


def heads_first(matrix):
    return matrix.reshape(matrix.shape[0], HEADS, HEAD_DIM).transpose(1, 0, 2).astype(jnp.float32)


def heads_last(tensor):
    return tensor.transpose(1, 0, 2).reshape(tensor.shape[1], HEADS * HEAD_DIM)


def halfway(tensor):
    return lax.optimization_barrier(tensor.astype(jnp.bfloat16)).astype(jnp.float32)


def reference(query_rows, key_rows, value_rows, out_grad, random_blocks, global_blocks):
    full_width = HEADS * HEAD_DIM
    scale_factor = HEAD_DIM ** -0.5
    part_count = 3 + RANDOM + GLOBALS
    empty_block = jnp.zeros((1, BLOCK, full_width), jnp.bfloat16)
    key_padded = jnp.concatenate([empty_block, key_rows.reshape(NBLK, BLOCK, full_width), empty_block], axis=0)
    value_padded = jnp.concatenate([empty_block, value_rows.reshape(NBLK, BLOCK, full_width), empty_block], axis=0)
    query_blocks = query_rows.reshape(NBLK, BLOCK, full_width)
    grad_blocks = out_grad.reshape(NBLK, BLOCK, full_width)
    part_iota = jnp.arange(part_count, dtype=jnp.int32)
    random_part = (part_iota >= 3) & (part_iota < 3 + RANDOM)

    def one_block(carry, which):
        key_sum, value_sum = carry
        picked_ids = jnp.concatenate([which + jnp.arange(3, dtype=jnp.int32), random_blocks[which].astype(jnp.int32) + 1, global_blocks.astype(jnp.int32) + 1]).astype(jnp.int32)
        part_ok = jnp.ones((part_count,), jnp.bool_).at[0].set(which > 0).at[2].set(which < NBLK - 1)
        key_ok = jnp.repeat(part_ok, BLOCK)
        query_heads = heads_first(query_blocks[which])
        grad_heads = heads_first(grad_blocks[which])
        key_heads = heads_first(key_padded[picked_ids].reshape(part_count * BLOCK, full_width))
        value_heads = heads_first(value_padded[picked_ids].reshape(part_count * BLOCK, full_width))
        scores = jnp.einsum("hqd,hkd->hqk", query_heads, key_heads) * scale_factor
        scores = jnp.where(key_ok[None, None, :], scores, masked_score)
        row_max = jnp.max(scores, axis=-1, keepdims=True)
        weights_raw = jnp.exp(scores - row_max)
        probabilities = weights_raw / jnp.sum(weights_raw, axis=-1, keepdims=True)
        probs_half = halfway(probabilities)
        attended = jnp.einsum("hqk,hkd->hqd", probs_half, value_heads)
        prob_grad = jnp.einsum("hqd,hkd->hqk", grad_heads, value_heads)
        row_delta = jnp.sum(grad_heads * attended, axis=-1, keepdims=True)
        score_grad = halfway(probabilities * (prob_grad - row_delta))
        query_grad = jnp.einsum("hqk,hkd->hqd", score_grad, key_heads) * scale_factor
        key_grad = heads_last(jnp.einsum("hqk,hqd->hkd", score_grad, query_heads) * scale_factor).reshape(part_count, BLOCK, full_width)
        value_grad = heads_last(jnp.einsum("hqk,hqd->hkd", probs_half, grad_heads)).reshape(part_count, BLOCK, full_width)
        key_grad = jnp.where(random_part[:, None, None], halfway(key_grad), key_grad)
        value_grad = jnp.where(random_part[:, None, None], halfway(value_grad), value_grad)
        key_sum = key_sum.at[picked_ids].add(key_grad)
        value_sum = value_sum.at[picked_ids].add(value_grad)
        return (key_sum, value_sum), (heads_last(attended).astype(jnp.bfloat16), heads_last(query_grad).astype(jnp.bfloat16))

    start_sum = jnp.zeros((NBLK + 2, BLOCK, full_width), jnp.float32)
    (key_sum, value_sum), (attended_all, query_all) = lax.scan(one_block, (start_sum, start_sum), jnp.arange(NBLK, dtype=jnp.int32))
    attn_out = attended_all.reshape(SEQLEN, full_width)
    q_grad = query_all.reshape(SEQLEN, full_width)
    k_grad = key_sum[1:NBLK + 1].reshape(SEQLEN, full_width).astype(jnp.bfloat16)
    v_grad = value_sum[1:NBLK + 1].reshape(SEQLEN, full_width).astype(jnp.bfloat16)
    return (attn_out, q_grad, k_grad, v_grad)
```

```python
import jax
import jax.numpy as jnp
from jax import lax
from jax.experimental import pallas as pl
from jax.experimental.pallas import tpu as pltpu
from jax.sharding import Mesh
from jax.sharding import PartitionSpec as P

HEAD_DIM = 64
BLOCK = 64
LANES = 128
COLUMN = 16
CHIPS = 32
RANDOMS = 32
UNITS = 40
ROWS = 2
SCALE = HEAD_DIM**-0.5
VMEM = 48 * 1024 * 1024


def vmem_call(kernel, out_shape, scratch=(), **specs):
    return pl.pallas_call(
        kernel,
        out_shape=out_shape,
        scratch_shapes=scratch,
        compiler_params=pltpu.CompilerParams(vmem_limit_bytes=VMEM),
        **specs,
    )


def low_lanes(shape):
    return lax.broadcasted_iota(jnp.int32, shape, len(shape) - 1) < HEAD_DIM


def pack_kernel(q_ref, g_ref, k_ref, v_ref, out_ref):
    low = low_lanes((BLOCK, LANES))
    for row, (a_ref, b_ref) in enumerate(((q_ref, g_ref), (k_ref, v_ref))):
        rows = slice(row * BLOCK, (row + 1) * BLOCK)
        for pair in range(COLUMN // 2):
            lanes = slice(pair * LANES, (pair + 1) * LANES)
            a = a_ref[:, lanes].astype(jnp.float32)
            b = b_ref[:, lanes].astype(jnp.float32)
            a_turned = pltpu.roll(a, HEAD_DIM, 1)
            b_turned = pltpu.roll(b, HEAD_DIM, 1)
            out_ref[2 * pair, rows, :] = jnp.where(low, a, b_turned).astype(jnp.bfloat16)
            out_ref[2 * pair + 1, rows, :] = jnp.where(low, a_turned, b).astype(jnp.bfloat16)


def unpack_kernel(in_ref, o_ref, dq_ref, dk_ref, dv_ref):
    low = low_lanes((BLOCK, LANES))
    for row, (a_ref, b_ref) in enumerate(((dq_ref, o_ref), (dk_ref, dv_ref))):
        rows = slice(row * BLOCK, (row + 1) * BLOCK)
        for pair in range(COLUMN // 2):
            lanes = slice(pair * LANES, (pair + 1) * LANES)
            even = in_ref[2 * pair, rows, :].astype(jnp.float32)
            odd = in_ref[2 * pair + 1, rows, :].astype(jnp.float32)
            even_turned = pltpu.roll(even, HEAD_DIM, 1)
            odd_turned = pltpu.roll(odd, HEAD_DIM, 1)
            a_ref[:, lanes] = jnp.where(low, even, odd_turned).astype(jnp.bfloat16)
            b_ref[:, lanes] = jnp.where(low, even_turned, odd).astype(jnp.bfloat16)


def attend_kernel(edge_ref, own_ref, unit_ref, out_ref, grad_ref, own_grad_ref, edge_grad):
    low = low_lanes((BLOCK, LANES))
    key_low = low_lanes((7 * BLOCK, LANES))
    key_part = lax.broadcasted_iota(jnp.int32, (BLOCK, 7 * BLOCK), 1) // BLOCK
    zero = jnp.zeros((BLOCK, LANES), jnp.bfloat16)
    own_grad_ref[...] = jnp.zeros(own_grad_ref.shape, jnp.float32)
    edge_grad[...] = jnp.zeros(edge_grad.shape, jnp.float32)

    def own_key(block):
        if block < 0:
            return unit_ref[RANDOMS + 2]
        if block >= COLUMN:
            return unit_ref[RANDOMS + 3]
        return own_ref[block, BLOCK:, :]

    for block in range(COLUMN):
        pair = own_ref[block, :BLOCK, :]
        rows = jnp.concatenate([jnp.where(low, pair, zero), jnp.where(low, zero, pair)], axis=0)
        keys = jnp.concatenate(
            [
                own_key(block - 1),
                own_key(block),
                own_key(block + 1),
                unit_ref[2 * block],
                unit_ref[2 * block + 1],
                unit_ref[RANDOMS],
                unit_ref[RANDOMS + 1],
            ],
            axis=0,
        )
        both = lax.dot_general(
            rows, keys, (((1,), (1,)), ((), ())), preferred_element_type=jnp.float32
        )
        scores = both[:BLOCK] * SCALE
        prob_grad = both[BLOCK:]
        if block == 0:
            scores = jnp.where((key_part == 0) & (edge_ref[0] != 0), -1e30, scores)
        if block == COLUMN - 1:
            scores = jnp.where((key_part == 2) & (edge_ref[1] != 0), -1e30, scores)
        raised = jnp.exp(scores - jnp.max(scores, axis=1, keepdims=True))
        probabilities = raised / jnp.sum(raised, axis=1, keepdims=True)
        probs_half = probabilities.astype(jnp.bfloat16)
        row_delta = jnp.sum(probs_half.astype(jnp.float32) * prob_grad, axis=1, keepdims=True)
        score_grad = (probabilities * (prob_grad - row_delta)).astype(jnp.bfloat16)
        stacked = jnp.concatenate([score_grad, probs_half], axis=0)
        mixed = jnp.dot(stacked, keys, preferred_element_type=jnp.float32)
        out_ref[block] = jnp.where(low, mixed[:BLOCK] * SCALE, mixed[BLOCK:]).astype(jnp.bfloat16)
        part = lax.dot_general(
            stacked, rows, (((0,), (0,)), ((), ())), preferred_element_type=jnp.float32
        )
        part = jnp.where(key_low, part * SCALE, part)
        for step in range(3):
            grad = part[step * BLOCK : (step + 1) * BLOCK]
            where = block + step - 1
            if where < 0:
                grad_ref[RANDOMS + 2] = grad.astype(jnp.bfloat16)
            elif where >= COLUMN:
                grad_ref[RANDOMS + 3] = grad.astype(jnp.bfloat16)
            else:
                own_grad_ref[where] += grad
        for step in range(2):
            grad_ref[2 * block + step] = part[(3 + step) * BLOCK : (4 + step) * BLOCK].astype(
                jnp.bfloat16
            )
            edge_grad[step] += part[(5 + step) * BLOCK : (6 + step) * BLOCK]
    for step in range(2):
        grad_ref[RANDOMS + step] = edge_grad[step].astype(jnp.bfloat16)
    for unit in range(RANDOMS + 4, UNITS):
        grad_ref[unit] = zero


def swap(value, axis):
    return lax.all_to_all(value, axis, split_axis=0, concat_axis=0, tiled=True)


def body(query_rows, key_rows, value_rows, out_grad, random_blocks, global_blocks):
    chip, core = lax.axis_index("chip"), lax.axis_index("core")
    half = jnp.bfloat16
    column = ("core", "head")

    packed = vmem_call(pack_kernel, jax.ShapeDtypeStruct((COLUMN, 2 * BLOCK, LANES), half))(
        query_rows, out_grad, key_rows, value_rows
    )
    own = swap(packed, column)

    other = lax.ppermute(random_blocks, "core", [(0, 1), (1, 0)])
    mine = random_blocks.reshape(1, -1)
    other = other.reshape(1, -1)
    named = jnp.where(
        core == 0, jnp.concatenate([mine, other], 1), jnp.concatenate([other, mine], 1)
    )
    named = jnp.concatenate([named // 8, named % 8], 0).astype(half)
    named = jnp.pad(named, ((0, 6), (0, LANES - RANDOMS)))

    spread = own[:, BLOCK:].reshape(COLUMN, ROWS, CHIPS, LANES).transpose(2, 1, 0, 3)
    spread = spread.reshape(CHIPS, ROWS * COLUMN, LANES)
    spread = jnp.concatenate([spread, jnp.broadcast_to(named[None], (CHIPS, 8, LANES))], axis=1)
    held = swap(spread, "chip")

    blocks = CHIPS * COLUMN
    table = jnp.concatenate(
        [held[:, r * COLUMN : (r + 1) * COLUMN].reshape(blocks, LANES) for r in range(ROWS)], axis=1
    )
    ids = held[:, 2 * COLUMN : 2 * COLUMN + 2, :RANDOMS].astype(jnp.float32)
    ids = (ids[:, 0] * 8 + ids[:, 1]).astype(jnp.int32)
    first = jnp.arange(CHIPS, dtype=jnp.int32)[:, None] * COLUMN
    ids = jnp.concatenate(
        [
            ids,
            jnp.broadcast_to(global_blocks[None], (CHIPS, 2)),
            first - 1,
            jnp.where(first + COLUMN < blocks, first + COLUMN, -1),
            jnp.full((CHIPS, UNITS - RANDOMS - 4), -1, jnp.int32),
        ],
        axis=1,
    ).reshape(-1)
    block_iota = jnp.arange(blocks, dtype=jnp.int32)
    pick = (ids[:, None] == block_iota[None, :]).astype(half)
    sent = jnp.dot(pick, table, preferred_element_type=jnp.float32).astype(half)
    units = swap(sent.reshape(CHIPS, UNITS, ROWS * LANES), "chip")
    units = units.reshape(CHIPS, UNITS, ROWS, LANES).transpose(1, 2, 0, 3)
    units = units.reshape(UNITS, BLOCK, LANES)

    edges = jnp.stack([chip == 0, chip == CHIPS - 1]).astype(jnp.int32)
    outs, unit_grad, own_grad = vmem_call(
        attend_kernel,
        (
            jax.ShapeDtypeStruct((COLUMN, BLOCK, LANES), half),
            jax.ShapeDtypeStruct((UNITS, BLOCK, LANES), half),
            jax.ShapeDtypeStruct((COLUMN, BLOCK, LANES), jnp.float32),
        ),
        [pltpu.VMEM((2, BLOCK, LANES), jnp.float32)],
        in_specs=[pl.BlockSpec(memory_space=pltpu.SMEM)] + [pl.BlockSpec(memory_space=pltpu.VMEM)] * 2,
    )(edges, own, units)

    back = unit_grad.reshape(UNITS, ROWS, CHIPS, LANES).transpose(2, 0, 1, 3)
    back = swap(back.reshape(CHIPS, UNITS, ROWS * LANES), "chip").reshape(-1, ROWS * LANES)
    place = (block_iota[:, None] == ids[None, :]).astype(half)
    total = jnp.dot(place, back, preferred_element_type=jnp.float32).astype(half)
    total = swap(total.reshape(CHIPS, COLUMN, ROWS * LANES), "chip")
    total = total.reshape(CHIPS, COLUMN, ROWS, LANES).transpose(1, 2, 0, 3)
    total = total.reshape(COLUMN, BLOCK, LANES).astype(jnp.float32)
    pair_grad = (own_grad + total).astype(half)
    result = swap(jnp.concatenate([outs, pair_grad], axis=1), column)
    return vmem_call(unpack_kernel, (jax.ShapeDtypeStruct(query_rows.shape, half),) * 4)(result)


def solution(mesh):
    columns = Mesh(mesh.devices.reshape(CHIPS, 2, COLUMN // 2), ("chip", "core", "head"))
    rows = P(("chip", "core", "head"), None)
    return jax.shard_map(
        body,
        mesh=columns,
        in_specs=(rows, rows, rows, rows, P(("chip", "core"), None), P()),
        out_specs=(rows, rows, rows, rows),
        check_vma=False,
    )
```

```python
import math

import jax
import jax.numpy as jnp
from jax import lax
from jax.experimental import pallas as pl
from jax.experimental.pallas import tpu as pltpu
from jax.sharding import Mesh
from jax.sharding import PartitionSpec as P

HEAD_DIM = 64
BLOCK = 64
LANES = 128
COLUMN = 16
COLUMNS = 32
RANDOMS = 32
PARTNER = RANDOMS + 2
EDGE = PARTNER + COLUMN
USED = EDGE + 4
UNITS = 56
ROWS = 2
ID_ROWS = 8
GROUP = 8
SCALE = HEAD_DIM**-0.5
EXP2_SCALE = SCALE * math.log2(math.e)
VMEM = 48 * 1024 * 1024
WHOLE_VMEM = 60 * 1024 * 1024


def vmem_call(kernel, out_shape, scratch=(), vmem=VMEM, **specs):
    return pl.pallas_call(
        kernel,
        out_shape=out_shape,
        scratch_shapes=scratch,
        compiler_params=pltpu.CompilerParams(vmem_limit_bytes=vmem),
        **specs,
    )


def low_lanes(shape):
    return lax.broadcasted_iota(jnp.int32, shape, len(shape) - 1) < HEAD_DIM


def pack_kernel(random_ref, q_ref, g_ref, k_ref, v_ref, out_ref, held, arrived):
    copies = [
        pltpu.make_async_copy(ref, held.at[i], arrived.at[i])
        for i, ref in enumerate((q_ref, g_ref, k_ref, v_ref))
    ]
    for copy in copies:
        copy.start()
    yh, zh, zl = (lax.axis_index(axis) for axis in ("yh", "zh", "zl"))
    low = low_lanes((BLOCK, LANES))
    lane = lax.broadcasted_iota(jnp.int32, (ID_ROWS, LANES), 1)
    ids = jnp.zeros((ID_ROWS, LANES), jnp.int32)
    for step in range(2):
        name = random_ref[step, 2 * zh + zl]
        at = 2 * (4 * yh + zh) + step
        ids = jnp.where(lane == at, lax.shift_right_logical(name, 3), ids)
        ids = jnp.where(lane == at + RANDOMS, jnp.bitwise_and(name, 7), ids)
    ids = ids.astype(jnp.float32).astype(jnp.bfloat16)
    for rank in range(COLUMN):
        out_ref[rank, 2 * BLOCK :, :] = ids
    for row in range(2):
        copies[2 * row].wait()
        copies[2 * row + 1].wait()
        rows = slice(row * BLOCK, (row + 1) * BLOCK)
        for pair in range(COLUMN // 2):
            lanes = slice(pair * LANES, (pair + 1) * LANES)
            a = held[2 * row, :, lanes].astype(jnp.float32)
            b = held[2 * row + 1, :, lanes].astype(jnp.float32)
            a_turned = pltpu.roll(a, HEAD_DIM, 1)
            b_turned = pltpu.roll(b, HEAD_DIM, 1)
            out_ref[2 * pair, rows, :] = jnp.where(low, a, b_turned).astype(jnp.bfloat16)
            out_ref[2 * pair + 1, rows, :] = jnp.where(low, a_turned, b).astype(jnp.bfloat16)


def unpack_kernel(in_ref, o_ref, dq_ref, dk_ref, dv_ref):
    low = low_lanes((BLOCK, LANES))
    for row, (a_ref, b_ref) in enumerate(((dq_ref, o_ref), (dk_ref, dv_ref))):
        rows = slice(row * BLOCK, (row + 1) * BLOCK)
        for pair in range(COLUMN // 2):
            lanes = slice(pair * LANES, (pair + 1) * LANES)
            even = in_ref[2 * pair, rows, :].astype(jnp.float32)
            odd = in_ref[2 * pair + 1, rows, :].astype(jnp.float32)
            even_turned = pltpu.roll(even, HEAD_DIM, 1)
            odd_turned = pltpu.roll(odd, HEAD_DIM, 1)
            a_ref[:, lanes] = jnp.where(low, even, odd_turned).astype(jnp.bfloat16)
            b_ref[:, lanes] = jnp.where(low, even_turned, odd).astype(jnp.bfloat16)


def attend_kernel(flag_ref, own_ref, unit_ref, out_ref, grad_ref, own_grad_ref, shared, near, far):
    low = low_lanes((BLOCK, LANES))
    key_low = low_lanes((7 * BLOCK, LANES))
    far_keys = lax.broadcasted_iota(jnp.int32, (1, 7 * BLOCK), 1) // BLOCK == 2
    zero = jnp.zeros((BLOCK, LANES), jnp.bfloat16)
    odd = flag_ref[2] != 0
    shared[...] = jnp.zeros(shared.shape, jnp.float32)

    def far_key(block):
        before = block - 1 + PARTNER if block % 4 > 0 else EDGE + block // 4
        after = block + 1 + PARTNER if block % 4 < 3 else EDGE + block // 4
        return jnp.where(odd, unit_ref[after], unit_ref[before])

    for start in range(0, COLUMN, GROUP):
        group = range(start, start + GROUP)
        rows, keys, both, stacked = {}, {}, {}, {}
        for block in group:
            pair = own_ref[block, :BLOCK, :]
            rows[block] = jnp.concatenate(
                [jnp.where(low, pair, zero), jnp.where(low, zero, pair)], axis=0
            )
            keys[block] = jnp.concatenate(
                [
                    own_ref[block, BLOCK : 2 * BLOCK, :],
                    unit_ref[PARTNER + block],
                    far_key(block),
                    unit_ref[2 * block],
                    unit_ref[2 * block + 1],
                    unit_ref[RANDOMS],
                    unit_ref[RANDOMS + 1],
                ],
                axis=0,
            )
            both[block] = lax.dot_general(
                rows[block],
                keys[block],
                (((1,), (1,)), ((), ())),
                preferred_element_type=jnp.float32,
            )
        for block in group:
            scores, prob_grad = both[block][:BLOCK], both[block][BLOCK:]
            if block == 0:
                scores = jnp.where(far_keys & (flag_ref[0] != 0), -1e30, scores)
            if block == COLUMN - 1:
                scores = jnp.where(far_keys & (flag_ref[1] != 0), -1e30, scores)
            raised = jnp.exp2((scores - jnp.max(scores, axis=1, keepdims=True)) * EXP2_SCALE)
            probabilities = raised * (1.0 / jnp.sum(raised, axis=1, keepdims=True))
            probs_half = probabilities.astype(jnp.bfloat16)
            row_delta = jnp.sum(probs_half.astype(jnp.float32) * prob_grad, axis=1, keepdims=True)
            score_grad = (probabilities * (prob_grad - row_delta)).astype(jnp.bfloat16)
            stacked[block] = jnp.concatenate([score_grad, probs_half], axis=0)
        for block in group:
            mixed = jnp.dot(stacked[block], keys[block], preferred_element_type=jnp.float32)
            out_ref[block] = jnp.where(low, mixed[:BLOCK] * SCALE, mixed[BLOCK:]).astype(
                jnp.bfloat16
            )
            part = lax.dot_general(
                stacked[block],
                rows[block],
                (((0,), (0,)), ((), ())),
                preferred_element_type=jnp.float32,
            )
            part = jnp.where(key_low, part * SCALE, part)
            own_grad_ref[block] = part[:BLOCK]
            near[block] = part[BLOCK : 2 * BLOCK]
            far[block] = part[2 * BLOCK : 3 * BLOCK]
            for step in range(2):
                grad_ref[2 * block + step] = part[(3 + step) * BLOCK : (4 + step) * BLOCK].astype(
                    jnp.bfloat16
                )
                shared[step] += part[(5 + step) * BLOCK : (6 + step) * BLOCK]
    for step in range(2):
        grad_ref[RANDOMS + step] = shared[step].astype(jnp.bfloat16)
    none = jnp.zeros((BLOCK, LANES), jnp.float32)
    for block in range(COLUMN):
        after = far[block + 1] if block % 4 < 3 else none
        before = far[block - 1] if block % 4 > 0 else none
        grad_ref[PARTNER + block] = (near[block] + jnp.where(odd, before, after)).astype(
            jnp.bfloat16
        )
    for run in range(4):
        edge = jnp.where(odd, far[4 * run + 3], far[4 * run])
        grad_ref[EDGE + run] = edge.astype(jnp.bfloat16)
    for unit in range(USED, UNITS):
        grad_ref[unit] = zero


def swap(value, axis):
    return lax.all_to_all(value, axis, split_axis=0, concat_axis=0, tiled=True)


def body(query_rows, key_rows, value_rows, out_grad, random_blocks, global_blocks):
    half = jnp.bfloat16
    column, plane = ("yh", "zh"), ("x", "yl", "zl", "core")
    blocks = COLUMNS * COLUMN
    odd = lax.axis_index("zl")
    my_column = lax.axis_index(plane)

    columns = jnp.arange(COLUMNS, dtype=jnp.int32)[:, None]
    places = jnp.arange(COLUMN, dtype=jnp.int32)[None]
    numbers = (
        columns // 8 * 128
        + columns // 4 % 2 * 16
        + columns % 2 * 8
        + columns // 2 % 2
        + places // 4 * 32
        + places % 4 * 2
    )
    odd_column = columns // 2 % 2
    partners = numbers + 1 - 2 * odd_column
    edges = jnp.where(odd_column == 1, numbers[:, 3::4] + 1, numbers[:, 0::4] - 1)

    smem, hbm = pl.BlockSpec(memory_space=pltpu.SMEM), pl.BlockSpec(memory_space=pltpu.HBM)
    vmem = pl.BlockSpec(memory_space=pltpu.VMEM)
    packed = vmem_call(
        pack_kernel,
        jax.ShapeDtypeStruct((COLUMN, 2 * BLOCK + ID_ROWS, LANES), half),
        [pltpu.VMEM((4, *query_rows.shape), half), pltpu.SemaphoreType.DMA((4,))],
        vmem=WHOLE_VMEM,
        in_specs=[smem] + [hbm] * 4,
    )(random_blocks.T, query_rows, out_grad, key_rows, value_rows)
    own = swap(packed, column)

    spread = own[:, BLOCK : 2 * BLOCK].reshape(COLUMN, ROWS, COLUMNS, LANES).transpose(2, 1, 0, 3)
    spread = spread.reshape(COLUMNS, ROWS * COLUMN, LANES)
    named = jnp.sum(own[:, 2 * BLOCK :].astype(jnp.float32), axis=0).astype(half)
    named = jnp.broadcast_to(named[None], (COLUMNS, ID_ROWS, LANES))
    held = swap(jnp.concatenate([spread, named], axis=1), plane)

    table = jnp.concatenate(
        [held[:, r * COLUMN : (r + 1) * COLUMN].reshape(blocks, LANES) for r in range(ROWS)], axis=1
    )
    ids = held[:, ROWS * COLUMN, : 2 * RANDOMS].astype(jnp.float32)
    ids = (ids[:, :RANDOMS] * 8 + ids[:, RANDOMS:]).astype(jnp.int32)
    shared = jnp.broadcast_to(global_blocks[None], (COLUMNS, 2))
    unused = jnp.full((COLUMNS, UNITS - USED), -1, jnp.int32)
    ids = jnp.concatenate([ids, shared, partners, edges, unused], axis=1).reshape(-1)
    numbers = numbers.reshape(-1)
    pick = (ids[:, None] == numbers[None, :]).astype(half)
    sent = jnp.dot(pick, table, preferred_element_type=jnp.float32).astype(half)
    units = swap(sent.reshape(COLUMNS, UNITS, ROWS * LANES), plane)
    units = units.reshape(COLUMNS, UNITS, ROWS, LANES).transpose(1, 2, 0, 3)
    units = units.reshape(UNITS, BLOCK, LANES)

    flags = jnp.stack([my_column == 0, my_column == COLUMNS - 1, odd == 1]).astype(jnp.int32)
    outs, unit_grad, own_grad = vmem_call(
        attend_kernel,
        (
            jax.ShapeDtypeStruct((COLUMN, BLOCK, LANES), half),
            jax.ShapeDtypeStruct((UNITS, BLOCK, LANES), half),
            jax.ShapeDtypeStruct((COLUMN, BLOCK, LANES), jnp.float32),
        ),
        [pltpu.VMEM((count, BLOCK, LANES), jnp.float32) for count in (2, COLUMN, COLUMN)],
        in_specs=[smem, vmem, vmem],
    )(flags, own, units)

    back = unit_grad.reshape(UNITS, ROWS, COLUMNS, LANES).transpose(2, 0, 1, 3)
    back = swap(back.reshape(COLUMNS, UNITS, ROWS * LANES), plane).reshape(-1, ROWS * LANES)
    place = (numbers[:, None] == ids[None, :]).astype(half)
    total = jnp.dot(place, back, preferred_element_type=jnp.float32).astype(half)
    total = swap(total.reshape(COLUMNS, COLUMN, ROWS * LANES), plane)
    total = total.reshape(COLUMNS, COLUMN, ROWS, LANES).transpose(1, 2, 0, 3)
    total = total.reshape(COLUMN, BLOCK, LANES).astype(jnp.float32)
    pair_grad = (own_grad + total).astype(half)
    result = swap(jnp.concatenate([outs, pair_grad], axis=1), column)
    return vmem_call(unpack_kernel, (jax.ShapeDtypeStruct(query_rows.shape, half),) * 4)(result)


def solution(mesh):
    split = Mesh(
        mesh.devices.reshape(4, 4, 2, 2, 4, 2), ("x", "yh", "yl", "core", "zh", "zl")
    )
    seq = ("x", "yh", "yl", "core")
    rows = P((*seq, "zh", "zl"), None)
    return jax.shard_map(
        body,
        mesh=split,
        in_specs=(rows, rows, rows, rows, P(seq, None), P()),
        out_specs=(rows, rows, rows, rows),
        check_vma=False,
    )
```

```python
import math

import jax
import jax.numpy as jnp
from jax import lax
from jax.experimental import pallas as pl
from jax.experimental.pallas import tpu as pltpu
from jax.sharding import Mesh
from jax.sharding import PartitionSpec as P

HEAD_DIM = 64
BLOCK = 64
LANES = 128
COLUMN = 16
COLUMNS = 32
RANDOMS = 32
PARTNER = RANDOMS + 2
EDGE = PARTNER + COLUMN
USED = EDGE + 4
UNITS = 56
ROWS = 2
ID_ROWS = 8
GROUP = 8
SCALE = HEAD_DIM**-0.5
EXP2_SCALE = SCALE * math.log2(math.e)
VMEM = 48 * 1024 * 1024
WHOLE_VMEM = 60 * 1024 * 1024


def vmem_call(kernel, out_shape, scratch=(), vmem=VMEM, **specs):
    return pl.pallas_call(
        kernel,
        out_shape=out_shape,
        scratch_shapes=scratch,
        compiler_params=pltpu.CompilerParams(vmem_limit_bytes=vmem),
        **specs,
    )


def low_lanes(shape):
    return lax.broadcasted_iota(jnp.int32, shape, len(shape) - 1) < HEAD_DIM


def pack_kernel(random_ref, q_ref, g_ref, k_ref, v_ref, out_ref, held, named, arrived):
    names = pltpu.make_async_copy(random_ref, named, arrived.at[4])
    copies = [
        pltpu.make_async_copy(ref, held.at[i], arrived.at[i])
        for i, ref in enumerate((q_ref, g_ref, k_ref, v_ref))
    ]
    names.start()
    for copy in copies:
        copy.start()
    yh, zh, zl = (lax.axis_index(axis) for axis in ("yh", "zh", "zl"))
    low = low_lanes((BLOCK, LANES))
    lane = lax.broadcasted_iota(jnp.int32, (ID_ROWS, LANES), 1)
    ids = jnp.zeros((ID_ROWS, LANES), jnp.int32)
    names.wait()
    for step in range(2):
        name = named[step, 2 * zh + zl]
        at = 2 * (4 * yh + zh) + step
        ids = jnp.where(lane == at, lax.shift_right_logical(name, 3), ids)
        ids = jnp.where(lane == at + RANDOMS, jnp.bitwise_and(name, 7), ids)
    ids = ids.astype(jnp.float32).astype(jnp.bfloat16)
    for rank in range(COLUMN):
        out_ref[rank, 2 * BLOCK :, :] = ids
    for row in range(2):
        copies[2 * row].wait()
        copies[2 * row + 1].wait()
        rows = slice(row * BLOCK, (row + 1) * BLOCK)
        for pair in range(COLUMN // 2):
            lanes = slice(pair * LANES, (pair + 1) * LANES)
            a = held[2 * row, :, lanes].astype(jnp.float32)
            b = held[2 * row + 1, :, lanes].astype(jnp.float32)
            a_turned = pltpu.roll(a, HEAD_DIM, 1)
            b_turned = pltpu.roll(b, HEAD_DIM, 1)
            out_ref[2 * pair, rows, :] = jnp.where(low, a, b_turned).astype(jnp.bfloat16)
            out_ref[2 * pair + 1, rows, :] = jnp.where(low, a_turned, b).astype(jnp.bfloat16)


def unpack_kernel(in_ref, o_ref, dq_ref, dk_ref, dv_ref):
    low = low_lanes((BLOCK, LANES))
    for row, (a_ref, b_ref) in enumerate(((dq_ref, o_ref), (dk_ref, dv_ref))):
        rows = slice(row * BLOCK, (row + 1) * BLOCK)
        for pair in range(COLUMN // 2):
            lanes = slice(pair * LANES, (pair + 1) * LANES)
            even = in_ref[2 * pair, rows, :].astype(jnp.float32)
            odd = in_ref[2 * pair + 1, rows, :].astype(jnp.float32)
            even_turned = pltpu.roll(even, HEAD_DIM, 1)
            odd_turned = pltpu.roll(odd, HEAD_DIM, 1)
            a_ref[:, lanes] = jnp.where(low, even, odd_turned).astype(jnp.bfloat16)
            b_ref[:, lanes] = jnp.where(low, even_turned, odd).astype(jnp.bfloat16)


def attend_kernel(flag_ref, own_ref, unit_ref, out_ref, grad_ref, own_grad_ref, shared, near, far):
    low = low_lanes((BLOCK, LANES))
    key_low = low_lanes((7 * BLOCK, LANES))
    far_keys = lax.broadcasted_iota(jnp.int32, (1, 7 * BLOCK), 1) // BLOCK == 2
    zero = jnp.zeros((BLOCK, LANES), jnp.bfloat16)
    odd = flag_ref[2] != 0
    shared[...] = jnp.zeros(shared.shape, jnp.float32)

    def far_key(block):
        before = block - 1 + PARTNER if block % 4 > 0 else EDGE + block // 4
        after = block + 1 + PARTNER if block % 4 < 3 else EDGE + block // 4
        return jnp.where(odd, unit_ref[after], unit_ref[before])

    for start in range(0, COLUMN, GROUP):
        group = range(start, start + GROUP)
        rows, keys, both, stacked = {}, {}, {}, {}
        for block in group:
            pair = own_ref[block, :BLOCK, :]
            rows[block] = jnp.concatenate(
                [jnp.where(low, pair, zero), jnp.where(low, zero, pair)], axis=0
            )
            keys[block] = jnp.concatenate(
                [
                    own_ref[block, BLOCK : 2 * BLOCK, :],
                    unit_ref[PARTNER + block],
                    far_key(block),
                    unit_ref[2 * block],
                    unit_ref[2 * block + 1],
                    unit_ref[RANDOMS],
                    unit_ref[RANDOMS + 1],
                ],
                axis=0,
            )
            both[block] = lax.dot_general(
                rows[block],
                keys[block],
                (((1,), (1,)), ((), ())),
                preferred_element_type=jnp.float32,
            )
        for block in group:
            scores, prob_grad = both[block][:BLOCK], both[block][BLOCK:]
            if block == 0:
                scores = jnp.where(far_keys & (flag_ref[0] != 0), -1e30, scores)
            if block == COLUMN - 1:
                scores = jnp.where(far_keys & (flag_ref[1] != 0), -1e30, scores)
            raised = jnp.exp2((scores - jnp.max(scores, axis=1, keepdims=True)) * EXP2_SCALE)
            probabilities = raised * (1.0 / jnp.sum(raised, axis=1, keepdims=True))
            probs_half = probabilities.astype(jnp.bfloat16)
            row_delta = jnp.sum(probs_half.astype(jnp.float32) * prob_grad, axis=1, keepdims=True)
            score_grad = (probabilities * (prob_grad - row_delta)).astype(jnp.bfloat16)
            stacked[block] = jnp.concatenate([score_grad, probs_half], axis=0)
        for block in group:
            mixed = jnp.dot(stacked[block], keys[block], preferred_element_type=jnp.float32)
            out_ref[block] = jnp.where(low, mixed[:BLOCK] * SCALE, mixed[BLOCK:]).astype(
                jnp.bfloat16
            )
            part = lax.dot_general(
                stacked[block],
                rows[block],
                (((0,), (0,)), ((), ())),
                preferred_element_type=jnp.float32,
            )
            part = jnp.where(key_low, part * SCALE, part)
            own_grad_ref[block] = part[:BLOCK]
            near[block] = part[BLOCK : 2 * BLOCK]
            far[block] = part[2 * BLOCK : 3 * BLOCK]
            for step in range(2):
                grad_ref[2 * block + step] = part[(3 + step) * BLOCK : (4 + step) * BLOCK].astype(
                    jnp.bfloat16
                )
                shared[step] += part[(5 + step) * BLOCK : (6 + step) * BLOCK]
    for step in range(2):
        grad_ref[RANDOMS + step] = shared[step].astype(jnp.bfloat16)
    none = jnp.zeros((BLOCK, LANES), jnp.float32)
    for block in range(COLUMN):
        after = far[block + 1] if block % 4 < 3 else none
        before = far[block - 1] if block % 4 > 0 else none
        grad_ref[PARTNER + block] = (near[block] + jnp.where(odd, before, after)).astype(
            jnp.bfloat16
        )
    for run in range(4):
        edge = jnp.where(odd, far[4 * run + 3], far[4 * run])
        grad_ref[EDGE + run] = edge.astype(jnp.bfloat16)
    for unit in range(USED, UNITS):
        grad_ref[unit] = zero


def swap(value, axis):
    return lax.all_to_all(value, axis, split_axis=0, concat_axis=0, tiled=True)


def body(query_rows, key_rows, value_rows, out_grad, random_blocks, global_blocks):
    half = jnp.bfloat16
    column, plane = ("yh", "zh"), ("x", "yl", "zl", "core")
    blocks = COLUMNS * COLUMN
    odd = lax.axis_index("zl")
    my_column = lax.axis_index(plane)

    columns = jnp.arange(COLUMNS, dtype=jnp.int32)[:, None]
    places = jnp.arange(COLUMN, dtype=jnp.int32)[None]
    numbers = (
        columns // 8 * 128
        + columns // 4 % 2 * 16
        + columns % 2 * 8
        + columns // 2 % 2
        + places // 4 * 32
        + places % 4 * 2
    )
    odd_column = columns // 2 % 2
    partners = numbers + 1 - 2 * odd_column
    edges = jnp.where(odd_column == 1, numbers[:, 3::4] + 1, numbers[:, 0::4] - 1)

    smem, hbm = pl.BlockSpec(memory_space=pltpu.SMEM), pl.BlockSpec(memory_space=pltpu.HBM)
    vmem = pl.BlockSpec(memory_space=pltpu.VMEM)
    packed = vmem_call(
        pack_kernel,
        jax.ShapeDtypeStruct((COLUMN, 2 * BLOCK + ID_ROWS, LANES), half),
        [
            pltpu.VMEM((4, *query_rows.shape), half),
            pltpu.SMEM(random_blocks.shape[::-1], jnp.int32),
            pltpu.SemaphoreType.DMA((5,)),
        ],
        vmem=WHOLE_VMEM,
        in_specs=[hbm] * 5,
    )(random_blocks.T, query_rows, out_grad, key_rows, value_rows)
    own = swap(packed, column)

    spread = own[:, BLOCK : 2 * BLOCK].reshape(COLUMN, ROWS, COLUMNS, LANES).transpose(2, 1, 0, 3)
    spread = spread.reshape(COLUMNS, ROWS * COLUMN, LANES)
    named = jnp.sum(own[:, 2 * BLOCK :].astype(jnp.float32), axis=0).astype(half)
    named = jnp.broadcast_to(named[None], (COLUMNS, ID_ROWS, LANES))
    held = swap(jnp.concatenate([spread, named], axis=1), plane)

    table = jnp.concatenate(
        [held[:, r * COLUMN : (r + 1) * COLUMN].reshape(blocks, LANES) for r in range(ROWS)], axis=1
    )
    ids = held[:, ROWS * COLUMN, : 2 * RANDOMS].astype(jnp.float32)
    ids = (ids[:, :RANDOMS] * 8 + ids[:, RANDOMS:]).astype(jnp.int32)
    shared = jnp.broadcast_to(global_blocks[None], (COLUMNS, 2))
    unused = jnp.full((COLUMNS, UNITS - USED), -1, jnp.int32)
    ids = jnp.concatenate([ids, shared, partners, edges, unused], axis=1).reshape(-1)
    numbers = numbers.reshape(-1)
    pick = (ids[:, None] == numbers[None, :]).astype(half)
    sent = jnp.dot(pick, table, preferred_element_type=jnp.float32).astype(half)
    units = swap(sent.reshape(COLUMNS, UNITS, ROWS * LANES), plane)
    units = units.reshape(COLUMNS, UNITS, ROWS, LANES).transpose(1, 2, 0, 3)
    units = units.reshape(UNITS, BLOCK, LANES)

    flags = jnp.stack([my_column == 0, my_column == COLUMNS - 1, odd == 1]).astype(jnp.int32)
    outs, unit_grad, own_grad = vmem_call(
        attend_kernel,
        (
            jax.ShapeDtypeStruct((COLUMN, BLOCK, LANES), half),
            jax.ShapeDtypeStruct((UNITS, BLOCK, LANES), half),
            jax.ShapeDtypeStruct((COLUMN, BLOCK, LANES), jnp.float32),
        ),
        [pltpu.VMEM((count, BLOCK, LANES), jnp.float32) for count in (2, COLUMN, COLUMN)],
        in_specs=[smem, vmem, vmem],
    )(flags, own, units)

    back = unit_grad.reshape(UNITS, ROWS, COLUMNS, LANES).transpose(2, 1, 0, 3)
    back = swap(back.reshape(COLUMNS, ROWS * UNITS, LANES), plane)
    place = (numbers[:, None] == ids[None, :]).astype(half)
    total = [
        jnp.dot(
            place,
            back[:, r * UNITS : (r + 1) * UNITS].reshape(-1, LANES),
            preferred_element_type=jnp.float32,
        )
        .astype(half)
        .reshape(COLUMNS, COLUMN, LANES)
        for r in range(ROWS)
    ]
    total = swap(jnp.concatenate(total, axis=1), plane)
    total = total.reshape(COLUMNS, ROWS, COLUMN, LANES).transpose(2, 1, 0, 3)
    total = total.reshape(COLUMN, BLOCK, LANES).astype(jnp.float32)
    pair_grad = (own_grad + total).astype(half)
    result = swap(jnp.concatenate([outs, pair_grad], axis=1), column)
    return vmem_call(unpack_kernel, (jax.ShapeDtypeStruct(query_rows.shape, half),) * 4)(result)


def solution(mesh):
    split = Mesh(
        mesh.devices.reshape(4, 4, 2, 2, 4, 2), ("x", "yh", "yl", "core", "zh", "zl")
    )
    seq = ("x", "yh", "yl", "core")
    rows = P((*seq, "zh", "zl"), None)
    return jax.shard_map(
        body,
        mesh=split,
        in_specs=(rows, rows, rows, rows, P(seq, None), P()),
        out_specs=(rows, rows, rows, rows),
        check_vma=False,
    )
```

```python
import math

import jax
import jax.numpy as jnp
import numpy as np
from jax import lax
from jax.experimental import pallas as pl
from jax.experimental.pallas import tpu as pltpu
from jax.sharding import Mesh
from jax.sharding import PartitionSpec as P

HEAD_DIM = 64
BLOCK = 64
LANES = 128
COLUMN = 16
COLUMNS = 32
RANDOMS = 32
PARTNER = RANDOMS + 2
EDGE = PARTNER + COLUMN
USED = EDGE + 4
UNITS = 56
ROWS = 2
ID_ROWS = 8
GROUP = 8
SCALE = HEAD_DIM**-0.5
EXP2_SCALE = SCALE * math.log2(math.e)
VMEM = 48 * 1024 * 1024
WHOLE_VMEM = 60 * 1024 * 1024


def vmem_call(kernel, out_shape, scratch=(), vmem=VMEM, **specs):
    return pl.pallas_call(
        kernel,
        out_shape=out_shape,
        scratch_shapes=scratch,
        compiler_params=pltpu.CompilerParams(vmem_limit_bytes=vmem),
        **specs,
    )


def low_lanes(shape):
    return lax.broadcasted_iota(jnp.int32, shape, len(shape) - 1) < HEAD_DIM


def pack_kernel(random_ref, q_ref, g_ref, k_ref, v_ref, out_ref, held, named, arrived):
    names = pltpu.make_async_copy(random_ref, named, arrived.at[4])
    copies = [
        pltpu.make_async_copy(ref, held.at[i], arrived.at[i])
        for i, ref in enumerate((q_ref, g_ref, k_ref, v_ref))
    ]
    names.start()
    for copy in copies:
        copy.start()
    yh, zh, zl = (lax.axis_index(axis) for axis in ("yh", "zh", "zl"))
    low = low_lanes((BLOCK, LANES))
    lane = lax.broadcasted_iota(jnp.int32, (ID_ROWS, LANES), 1)
    ids = jnp.zeros((ID_ROWS, LANES), jnp.int32)
    names.wait()
    for step in range(2):
        name = named[step, 2 * zh + zl]
        at = 2 * (4 * yh + zh) + step
        ids = jnp.where(lane == at, lax.shift_right_logical(name, 3), ids)
        ids = jnp.where(lane == at + RANDOMS, jnp.bitwise_and(name, 7), ids)
    ids = ids.astype(jnp.float32).astype(jnp.bfloat16)
    for rank in range(COLUMN):
        out_ref[rank, 2 * BLOCK :, :] = ids
    for row in range(2):
        copies[2 * row].wait()
        copies[2 * row + 1].wait()
        rows = slice(row * BLOCK, (row + 1) * BLOCK)
        for pair in range(COLUMN // 2):
            lanes = slice(pair * LANES, (pair + 1) * LANES)
            a = held[2 * row, :, lanes].astype(jnp.float32)
            b = held[2 * row + 1, :, lanes].astype(jnp.float32)
            a_turned = pltpu.roll(a, HEAD_DIM, 1)
            b_turned = pltpu.roll(b, HEAD_DIM, 1)
            out_ref[2 * pair, rows, :] = jnp.where(low, a, b_turned).astype(jnp.bfloat16)
            out_ref[2 * pair + 1, rows, :] = jnp.where(low, a_turned, b).astype(jnp.bfloat16)


def unpack_kernel(in_ref, o_ref, dq_ref, dk_ref, dv_ref):
    low = low_lanes((BLOCK, LANES))
    for row, (a_ref, b_ref) in enumerate(((dq_ref, o_ref), (dk_ref, dv_ref))):
        rows = slice(row * BLOCK, (row + 1) * BLOCK)
        for pair in range(COLUMN // 2):
            lanes = slice(pair * LANES, (pair + 1) * LANES)
            even = in_ref[2 * pair, rows, :].astype(jnp.float32)
            odd = in_ref[2 * pair + 1, rows, :].astype(jnp.float32)
            even_turned = pltpu.roll(even, HEAD_DIM, 1)
            odd_turned = pltpu.roll(odd, HEAD_DIM, 1)
            a_ref[:, lanes] = jnp.where(low, even, odd_turned).astype(jnp.bfloat16)
            b_ref[:, lanes] = jnp.where(low, even_turned, odd).astype(jnp.bfloat16)


def attend_kernel(own_ref, unit_ref, out_ref, grad_ref, own_grad_ref, shared, near, far):
    low = low_lanes((BLOCK, LANES))
    key_low = low_lanes((7 * BLOCK, LANES))
    far_keys = lax.broadcasted_iota(jnp.int32, (1, 7 * BLOCK), 1) // BLOCK == 2
    zero = jnp.zeros((BLOCK, LANES), jnp.bfloat16)
    x, yl, zl, core = (lax.axis_index(axis) for axis in ("x", "yl", "zl", "core"))
    column = 8 * x + 4 * yl + 2 * zl + core
    odd = zl == 1
    shared[...] = jnp.zeros(shared.shape, jnp.float32)

    def far_key(block):
        before = block - 1 + PARTNER if block % 4 > 0 else EDGE + block // 4
        after = block + 1 + PARTNER if block % 4 < 3 else EDGE + block // 4
        return jnp.where(odd, unit_ref[after], unit_ref[before])

    for start in range(0, COLUMN, GROUP):
        group = range(start, start + GROUP)
        rows, keys, both, stacked = {}, {}, {}, {}
        for block in group:
            pair = own_ref[block, :BLOCK, :]
            rows[block] = jnp.concatenate(
                [jnp.where(low, pair, zero), jnp.where(low, zero, pair)], axis=0
            )
            keys[block] = jnp.concatenate(
                [
                    own_ref[block, BLOCK : 2 * BLOCK, :],
                    unit_ref[PARTNER + block],
                    far_key(block),
                    unit_ref[2 * block],
                    unit_ref[2 * block + 1],
                    unit_ref[RANDOMS],
                    unit_ref[RANDOMS + 1],
                ],
                axis=0,
            )
            both[block] = lax.dot_general(
                rows[block],
                keys[block],
                (((1,), (1,)), ((), ())),
                preferred_element_type=jnp.float32,
            )
        for block in group:
            scores, prob_grad = both[block][:BLOCK], both[block][BLOCK:]
            if block == 0:
                scores = jnp.where(far_keys & (column == 0), -1e30, scores)
            if block == COLUMN - 1:
                scores = jnp.where(far_keys & (column == COLUMNS - 1), -1e30, scores)
            raised = jnp.exp2((scores - jnp.max(scores, axis=1, keepdims=True)) * EXP2_SCALE)
            probabilities = raised * (1.0 / jnp.sum(raised, axis=1, keepdims=True))
            probs_half = probabilities.astype(jnp.bfloat16)
            row_delta = jnp.sum(probs_half.astype(jnp.float32) * prob_grad, axis=1, keepdims=True)
            score_grad = (probabilities * (prob_grad - row_delta)).astype(jnp.bfloat16)
            stacked[block] = jnp.concatenate([score_grad, probs_half], axis=0)
        for block in group:
            mixed = jnp.dot(stacked[block], keys[block], preferred_element_type=jnp.float32)
            out_ref[block] = jnp.where(low, mixed[:BLOCK] * SCALE, mixed[BLOCK:]).astype(
                jnp.bfloat16
            )
            part = lax.dot_general(
                stacked[block],
                rows[block],
                (((0,), (0,)), ((), ())),
                preferred_element_type=jnp.float32,
            )
            part = jnp.where(key_low, part * SCALE, part)
            own_grad_ref[block] = part[:BLOCK]
            near[block] = part[BLOCK : 2 * BLOCK]
            far[block] = part[2 * BLOCK : 3 * BLOCK]
            for step in range(2):
                grad_ref[2 * block + step] = part[(3 + step) * BLOCK : (4 + step) * BLOCK].astype(
                    jnp.bfloat16
                )
                shared[step] += part[(5 + step) * BLOCK : (6 + step) * BLOCK]
    for step in range(2):
        grad_ref[RANDOMS + step] = shared[step].astype(jnp.bfloat16)
    none = jnp.zeros((BLOCK, LANES), jnp.float32)
    for block in range(COLUMN):
        after = far[block + 1] if block % 4 < 3 else none
        before = far[block - 1] if block % 4 > 0 else none
        grad_ref[PARTNER + block] = (near[block] + jnp.where(odd, before, after)).astype(
            jnp.bfloat16
        )
    for run in range(4):
        edge = jnp.where(odd, far[4 * run + 3], far[4 * run])
        grad_ref[EDGE + run] = edge.astype(jnp.bfloat16)
    for unit in range(USED, UNITS):
        grad_ref[unit] = zero


def swap(value, axis):
    return lax.all_to_all(value, axis, split_axis=0, concat_axis=0, tiled=True)


def body(query_rows, key_rows, value_rows, out_grad, random_blocks, global_blocks):
    half = jnp.bfloat16
    column, plane = ("yh", "zh"), ("x", "yl", "zl", "core")
    blocks = COLUMNS * COLUMN

    columns = np.arange(COLUMNS, dtype=np.int32)[:, None]
    places = np.arange(COLUMN, dtype=np.int32)[None]
    numbers = (
        columns // 8 * 128
        + columns // 4 % 2 * 16
        + columns % 2 * 8
        + columns // 2 % 2
        + places // 4 * 32
        + places % 4 * 2
    )
    odd_column = columns // 2 % 2
    partners = numbers + 1 - 2 * odd_column
    edges = np.where(odd_column == 1, numbers[:, 3::4] + 1, numbers[:, 0::4] - 1)

    hbm = pl.BlockSpec(memory_space=pltpu.HBM)
    vmem = pl.BlockSpec(memory_space=pltpu.VMEM)
    packed = vmem_call(
        pack_kernel,
        jax.ShapeDtypeStruct((COLUMN, 2 * BLOCK + ID_ROWS, LANES), half),
        [
            pltpu.VMEM((4, *query_rows.shape), half),
            pltpu.SMEM(random_blocks.shape[::-1], jnp.int32),
            pltpu.SemaphoreType.DMA((5,)),
        ],
        vmem=WHOLE_VMEM,
        in_specs=[hbm] * 5,
    )(random_blocks.T, query_rows, out_grad, key_rows, value_rows)
    own = swap(packed, column)

    spread = own[:, BLOCK : 2 * BLOCK].reshape(COLUMN, ROWS, COLUMNS, LANES).transpose(2, 1, 0, 3)
    spread = spread.reshape(COLUMNS, ROWS * COLUMN, LANES)
    named = jnp.sum(own[:, 2 * BLOCK :].astype(jnp.float32), axis=0).astype(half)
    named = jnp.broadcast_to(named[None], (COLUMNS, ID_ROWS, LANES))
    held = swap(jnp.concatenate([spread, named], axis=1), plane)

    held, global_blocks = lax.optimization_barrier((held, global_blocks))
    table = jnp.concatenate(
        [held[:, r * COLUMN : (r + 1) * COLUMN].reshape(blocks, LANES) for r in range(ROWS)], axis=1
    )
    ids = held[:, ROWS * COLUMN, : 2 * RANDOMS].astype(jnp.float32)
    ids = (ids[:, :RANDOMS] * 8 + ids[:, RANDOMS:]).astype(jnp.int32)
    shared = jnp.broadcast_to(global_blocks[None], (COLUMNS, 2))
    unused = np.full((COLUMNS, UNITS - USED), -1, np.int32)
    fixed = np.concatenate([partners, edges, unused], axis=1)
    ids = jnp.concatenate([ids, shared, fixed], axis=1).reshape(-1)
    numbers = numbers.reshape(-1)
    pick = (ids[:, None] == numbers[None, :]).astype(half)
    sent = jnp.dot(pick, table, preferred_element_type=jnp.float32).astype(half)
    units = swap(sent.reshape(COLUMNS, UNITS, ROWS * LANES), plane)
    units = units.reshape(COLUMNS, UNITS, ROWS, LANES).transpose(1, 2, 0, 3)
    units = units.reshape(UNITS, BLOCK, LANES)

    outs, unit_grad, own_grad = vmem_call(
        attend_kernel,
        (
            jax.ShapeDtypeStruct((COLUMN, BLOCK, LANES), half),
            jax.ShapeDtypeStruct((UNITS, BLOCK, LANES), half),
            jax.ShapeDtypeStruct((COLUMN, BLOCK, LANES), jnp.float32),
        ),
        [pltpu.VMEM((count, BLOCK, LANES), jnp.float32) for count in (2, COLUMN, COLUMN)],
        in_specs=[vmem, vmem],
    )(own, units)

    back = unit_grad.reshape(UNITS, ROWS, COLUMNS, LANES).transpose(2, 1, 0, 3)
    back = swap(back.reshape(COLUMNS, ROWS * UNITS, LANES), plane)
    place = (numbers[:, None] == ids[None, :]).astype(half)
    total = [
        jnp.dot(
            place,
            back[:, r * UNITS : (r + 1) * UNITS].reshape(-1, LANES),
            preferred_element_type=jnp.float32,
        )
        .astype(half)
        .reshape(COLUMNS, COLUMN, LANES)
        for r in range(ROWS)
    ]
    total = swap(jnp.concatenate(total, axis=1), plane)
    total = total.reshape(COLUMNS, ROWS, COLUMN, LANES).transpose(2, 1, 0, 3)
    total = total.reshape(COLUMN, BLOCK, LANES).astype(jnp.float32)
    pair_grad = (own_grad + total).astype(half)
    result = swap(jnp.concatenate([outs, pair_grad], axis=1), column)
    return vmem_call(unpack_kernel, (jax.ShapeDtypeStruct(query_rows.shape, half),) * 4)(result)


def solution(mesh):
    split = Mesh(
        mesh.devices.reshape(4, 4, 2, 2, 4, 2), ("x", "yh", "yl", "core", "zh", "zl")
    )
    seq = ("x", "yh", "yl", "core")
    rows = P((*seq, "zh", "zl"), None)
    return jax.shard_map(
        body,
        mesh=split,
        in_specs=(rows, rows, rows, rows, P(seq, None), P()),
        out_specs=(rows, rows, rows, rows),
        check_vma=False,
    )
```

```python
import math

import jax
import jax.numpy as jnp
import numpy as np
from jax import lax
from jax.experimental import pallas as pl
from jax.experimental.pallas import tpu as pltpu
from jax.sharding import Mesh
from jax.sharding import PartitionSpec as P

HEAD_DIM = 64
BLOCK = 64
LANES = 128
COLUMN = 16
COLUMNS = 32
RANDOMS = 32
PARTNER = RANDOMS + 2
EDGE = PARTNER + COLUMN
USED = EDGE + 4
UNITS = 56
ROWS = 2
ID_ROWS = 8
GROUP = 8
SCALE = HEAD_DIM**-0.5
EXP2_SCALE = SCALE * math.log2(math.e)
VMEM = 48 * 1024 * 1024
WHOLE_VMEM = 60 * 1024 * 1024


def vmem_call(kernel, out_shape, scratch=(), vmem=VMEM, **specs):
    return pl.pallas_call(
        kernel,
        out_shape=out_shape,
        scratch_shapes=scratch,
        compiler_params=pltpu.CompilerParams(vmem_limit_bytes=vmem),
        **specs,
    )


def low_lanes(shape):
    return lax.broadcasted_iota(jnp.int32, shape, len(shape) - 1) < HEAD_DIM


def pack_kernel(random_ref, q_ref, g_ref, k_ref, v_ref, out_ref, held, named, packed, arrived, left):
    names = pltpu.make_async_copy(random_ref, named, arrived.at[8])
    names.start()
    width, heads = held.shape[-1] // 2, COLUMN // 2
    copies, leaving = [], []
    for half in range(2):
        lanes = pl.ds(half * width, width)
        for i, ref in enumerate((q_ref, g_ref, k_ref, v_ref)):
            copy = pltpu.make_async_copy(
                ref.at[:, lanes], held.at[i, :, lanes], arrived.at[4 * half + i]
            )
            copy.start()
            copies.append(copy)
        ranks = pl.ds(half * heads, heads)
        leaving.append(
            pltpu.make_async_copy(packed.at[ranks], out_ref.at[ranks], left.at[half])
        )
    yh, zh, zl = (lax.axis_index(axis) for axis in ("yh", "zh", "zl"))
    low = low_lanes((BLOCK, LANES))
    lane = lax.broadcasted_iota(jnp.int32, (ID_ROWS, LANES), 1)
    ids = jnp.zeros((ID_ROWS, LANES), jnp.int32)
    names.wait()
    for step in range(2):
        name = named[step, 2 * zh + zl]
        at = 2 * (4 * yh + zh) + step
        ids = jnp.where(lane == at, lax.shift_right_logical(name, 3), ids)
        ids = jnp.where(lane == at + RANDOMS, jnp.bitwise_and(name, 7), ids)
    ids = ids.astype(jnp.float32).astype(jnp.bfloat16)
    for rank in range(COLUMN):
        packed[rank, 2 * BLOCK :, :] = ids
    for half in range(2):
        for copy in copies[4 * half : 4 * half + 4]:
            copy.wait()
        for pair in range(half * heads // 2, (half + 1) * heads // 2):
            lanes = slice(pair * LANES, (pair + 1) * LANES)
            for row in range(2):
                rows = slice(row * BLOCK, (row + 1) * BLOCK)
                a = held[2 * row, :, lanes].astype(jnp.float32)
                b = held[2 * row + 1, :, lanes].astype(jnp.float32)
                a_turned = pltpu.roll(a, HEAD_DIM, 1)
                b_turned = pltpu.roll(b, HEAD_DIM, 1)
                packed[2 * pair, rows, :] = jnp.where(low, a, b_turned).astype(jnp.bfloat16)
                packed[2 * pair + 1, rows, :] = jnp.where(low, a_turned, b).astype(jnp.bfloat16)
        leaving[half].start()
    for copy in leaving:
        copy.wait()


def unpack_kernel(in_ref, o_ref, dq_ref, dk_ref, dv_ref):
    low = low_lanes((BLOCK, LANES))
    for row, (a_ref, b_ref) in enumerate(((dq_ref, o_ref), (dk_ref, dv_ref))):
        rows = slice(row * BLOCK, (row + 1) * BLOCK)
        for pair in range(COLUMN // 2):
            lanes = slice(pair * LANES, (pair + 1) * LANES)
            even = in_ref[2 * pair, rows, :].astype(jnp.float32)
            odd = in_ref[2 * pair + 1, rows, :].astype(jnp.float32)
            even_turned = pltpu.roll(even, HEAD_DIM, 1)
            odd_turned = pltpu.roll(odd, HEAD_DIM, 1)
            a_ref[:, lanes] = jnp.where(low, even, odd_turned).astype(jnp.bfloat16)
            b_ref[:, lanes] = jnp.where(low, even_turned, odd).astype(jnp.bfloat16)


def attend_kernel(own_ref, unit_ref, out_ref, grad_ref, own_grad_ref, shared, near, far):
    low = low_lanes((BLOCK, LANES))
    key_low = low_lanes((7 * BLOCK, LANES))
    far_keys = lax.broadcasted_iota(jnp.int32, (1, 7 * BLOCK), 1) // BLOCK == 2
    zero = jnp.zeros((BLOCK, LANES), jnp.bfloat16)
    x, yl, zl, core = (lax.axis_index(axis) for axis in ("x", "yl", "zl", "core"))
    column = 8 * x + 4 * yl + 2 * zl + core
    odd = zl == 1
    shared[...] = jnp.zeros(shared.shape, jnp.float32)

    def far_key(block):
        before = block - 1 + PARTNER if block % 4 > 0 else EDGE + block // 4
        after = block + 1 + PARTNER if block % 4 < 3 else EDGE + block // 4
        return jnp.where(odd, unit_ref[after], unit_ref[before])

    for start in range(0, COLUMN, GROUP):
        group = range(start, start + GROUP)
        rows, keys, both, stacked = {}, {}, {}, {}
        for block in group:
            pair = own_ref[block, :BLOCK, :]
            rows[block] = jnp.concatenate(
                [jnp.where(low, pair, zero), jnp.where(low, zero, pair)], axis=0
            )
            keys[block] = jnp.concatenate(
                [
                    own_ref[block, BLOCK : 2 * BLOCK, :],
                    unit_ref[PARTNER + block],
                    far_key(block),
                    unit_ref[2 * block],
                    unit_ref[2 * block + 1],
                    unit_ref[RANDOMS],
                    unit_ref[RANDOMS + 1],
                ],
                axis=0,
            )
            both[block] = lax.dot_general(
                rows[block],
                keys[block],
                (((1,), (1,)), ((), ())),
                preferred_element_type=jnp.float32,
            )
        for block in group:
            scores, prob_grad = both[block][:BLOCK], both[block][BLOCK:]
            if block == 0:
                scores = jnp.where(far_keys & (column == 0), -1e30, scores)
            if block == COLUMN - 1:
                scores = jnp.where(far_keys & (column == COLUMNS - 1), -1e30, scores)
            raised = jnp.exp2((scores - jnp.max(scores, axis=1, keepdims=True)) * EXP2_SCALE)
            probabilities = raised * (1.0 / jnp.sum(raised, axis=1, keepdims=True))
            probs_half = probabilities.astype(jnp.bfloat16)
            row_delta = jnp.sum(probs_half.astype(jnp.float32) * prob_grad, axis=1, keepdims=True)
            score_grad = (probabilities * (prob_grad - row_delta)).astype(jnp.bfloat16)
            stacked[block] = jnp.concatenate([score_grad, probs_half], axis=0)
        for block in group:
            mixed = jnp.dot(stacked[block], keys[block], preferred_element_type=jnp.float32)
            out_ref[block] = jnp.where(low, mixed[:BLOCK] * SCALE, mixed[BLOCK:]).astype(
                jnp.bfloat16
            )
            part = lax.dot_general(
                stacked[block],
                rows[block],
                (((0,), (0,)), ((), ())),
                preferred_element_type=jnp.float32,
            )
            part = jnp.where(key_low, part * SCALE, part)
            own_grad_ref[block] = part[:BLOCK]
            near[block] = part[BLOCK : 2 * BLOCK]
            far[block] = part[2 * BLOCK : 3 * BLOCK]
            for step in range(2):
                grad_ref[2 * block + step] = part[(3 + step) * BLOCK : (4 + step) * BLOCK].astype(
                    jnp.bfloat16
                )
                shared[step] += part[(5 + step) * BLOCK : (6 + step) * BLOCK]
    for step in range(2):
        grad_ref[RANDOMS + step] = shared[step].astype(jnp.bfloat16)
    none = jnp.zeros((BLOCK, LANES), jnp.float32)
    for block in range(COLUMN):
        after = far[block + 1] if block % 4 < 3 else none
        before = far[block - 1] if block % 4 > 0 else none
        grad_ref[PARTNER + block] = (near[block] + jnp.where(odd, before, after)).astype(
            jnp.bfloat16
        )
    for run in range(4):
        edge = jnp.where(odd, far[4 * run + 3], far[4 * run])
        grad_ref[EDGE + run] = edge.astype(jnp.bfloat16)
    for unit in range(USED, UNITS):
        grad_ref[unit] = zero


def swap(value, axis):
    return lax.all_to_all(value, axis, split_axis=0, concat_axis=0, tiled=True)


def body(query_rows, key_rows, value_rows, out_grad, random_blocks, global_blocks):
    half = jnp.bfloat16
    column, plane = ("yh", "zh"), ("x", "yl", "zl", "core")
    blocks = COLUMNS * COLUMN

    columns = np.arange(COLUMNS, dtype=np.int32)[:, None]
    places = np.arange(COLUMN, dtype=np.int32)[None]
    numbers = (
        columns // 8 * 128
        + columns // 4 % 2 * 16
        + columns % 2 * 8
        + columns // 2 % 2
        + places // 4 * 32
        + places % 4 * 2
    )
    odd_column = columns // 2 % 2
    partners = numbers + 1 - 2 * odd_column
    edges = np.where(odd_column == 1, numbers[:, 3::4] + 1, numbers[:, 0::4] - 1)

    hbm = pl.BlockSpec(memory_space=pltpu.HBM)
    vmem = pl.BlockSpec(memory_space=pltpu.VMEM)
    packed = vmem_call(
        pack_kernel,
        jax.ShapeDtypeStruct((COLUMN, 2 * BLOCK + ID_ROWS, LANES), half),
        [
            pltpu.VMEM((4, *query_rows.shape), half),
            pltpu.SMEM(random_blocks.shape[::-1], jnp.int32),
            pltpu.VMEM((COLUMN, 2 * BLOCK + ID_ROWS, LANES), half),
            pltpu.SemaphoreType.DMA((9,)),
            pltpu.SemaphoreType.DMA((2,)),
        ],
        vmem=WHOLE_VMEM,
        in_specs=[hbm] * 5,
        out_specs=hbm,
    )(random_blocks.T, query_rows, out_grad, key_rows, value_rows)
    own = swap(packed, column)

    spread = own[:, BLOCK : 2 * BLOCK].reshape(COLUMN, ROWS, COLUMNS, LANES).transpose(2, 1, 0, 3)
    spread = spread.reshape(COLUMNS, ROWS * COLUMN, LANES)
    named = jnp.sum(own[:, 2 * BLOCK :].astype(jnp.float32), axis=0).astype(half)
    named = jnp.broadcast_to(named[None], (COLUMNS, ID_ROWS, LANES))
    held = swap(jnp.concatenate([spread, named], axis=1), plane)

    held, global_blocks = lax.optimization_barrier((held, global_blocks))
    table = jnp.concatenate(
        [held[:, r * COLUMN : (r + 1) * COLUMN].reshape(blocks, LANES) for r in range(ROWS)], axis=1
    )
    ids = held[:, ROWS * COLUMN, : 2 * RANDOMS].astype(jnp.float32)
    ids = (ids[:, :RANDOMS] * 8 + ids[:, RANDOMS:]).astype(jnp.int32)
    shared = jnp.broadcast_to(global_blocks[None], (COLUMNS, 2))
    unused = np.full((COLUMNS, UNITS - USED), -1, np.int32)
    fixed = np.concatenate([partners, edges, unused], axis=1)
    ids = jnp.concatenate([ids, shared, fixed], axis=1).reshape(-1)
    numbers = numbers.reshape(-1)
    pick = (ids[:, None] == numbers[None, :]).astype(half)
    sent = jnp.dot(pick, table, preferred_element_type=jnp.float32).astype(half)
    units = swap(sent.reshape(COLUMNS, UNITS, ROWS * LANES), plane)
    units = units.reshape(COLUMNS, UNITS, ROWS, LANES).transpose(1, 2, 0, 3)
    units = units.reshape(UNITS, BLOCK, LANES)

    outs, unit_grad, own_grad = vmem_call(
        attend_kernel,
        (
            jax.ShapeDtypeStruct((COLUMN, BLOCK, LANES), half),
            jax.ShapeDtypeStruct((UNITS, BLOCK, LANES), half),
            jax.ShapeDtypeStruct((COLUMN, BLOCK, LANES), jnp.float32),
        ),
        [pltpu.VMEM((count, BLOCK, LANES), jnp.float32) for count in (2, COLUMN, COLUMN)],
        in_specs=[vmem, vmem],
    )(own, units)

    back = unit_grad.reshape(UNITS, ROWS, COLUMNS, LANES).transpose(2, 0, 1, 3)
    back = swap(back.reshape(COLUMNS, UNITS, ROWS * LANES), plane).reshape(-1, ROWS * LANES)
    place = (numbers[:, None] == ids[None, :]).astype(half)
    total = jnp.dot(place, back, preferred_element_type=jnp.float32).astype(half)
    total = swap(total.reshape(COLUMNS, COLUMN, ROWS * LANES), plane)
    total = total.reshape(COLUMNS, COLUMN, ROWS, LANES).transpose(1, 2, 0, 3)
    total = total.reshape(COLUMN, BLOCK, LANES).astype(jnp.float32)
    pair_grad = (own_grad + total).astype(half)
    result = swap(jnp.concatenate([outs, pair_grad], axis=1), column)
    return vmem_call(unpack_kernel, (jax.ShapeDtypeStruct(query_rows.shape, half),) * 4)(result)


def solution(mesh):
    split = Mesh(
        mesh.devices.reshape(4, 4, 2, 2, 4, 2), ("x", "yh", "yl", "core", "zh", "zl")
    )
    seq = ("x", "yh", "yl", "core")
    rows = P((*seq, "zh", "zl"), None)
    return jax.shard_map(
        body,
        mesh=split,
        in_specs=(rows, rows, rows, rows, P(seq, None), P()),
        out_specs=(rows, rows, rows, rows),
        check_vma=False,
    )
```

```python
import math

import jax
import jax.numpy as jnp
import numpy as np
from jax import lax
from jax.experimental import pallas as pl
from jax.experimental.pallas import tpu as pltpu
from jax.sharding import Mesh
from jax.sharding import PartitionSpec as P

HEAD_DIM = 64
BLOCK = 64
LANES = 128
COLUMN = 16
COLUMNS = 32
RANDOMS = 32
PARTNER = RANDOMS + 2
EDGE = PARTNER + COLUMN
USED = EDGE + 4
UNITS = 56
ROWS = 2
ID_ROWS = 8
GROUP = 8
SCALE = HEAD_DIM**-0.5
EXP2_SCALE = SCALE * math.log2(math.e)
VMEM = 48 * 1024 * 1024
WHOLE_VMEM = 60 * 1024 * 1024


def vmem_call(kernel, out_shape, scratch=(), vmem=VMEM, **specs):
    return pl.pallas_call(
        kernel,
        out_shape=out_shape,
        scratch_shapes=scratch,
        compiler_params=pltpu.CompilerParams(vmem_limit_bytes=vmem),
        **specs,
    )


def low_lanes(shape):
    return lax.broadcasted_iota(jnp.int32, shape, len(shape) - 1) < HEAD_DIM


def pack_kernel(random_ref, q_ref, g_ref, k_ref, v_ref, out_ref, held, named, arrived):
    names = pltpu.make_async_copy(random_ref, named, arrived.at[4])
    copies = [
        pltpu.make_async_copy(ref, held.at[i], arrived.at[i])
        for i, ref in enumerate((q_ref, g_ref, k_ref, v_ref))
    ]
    names.start()
    for copy in copies:
        copy.start()
    yh, zh, zl = (lax.axis_index(axis) for axis in ("yh", "zh", "zl"))
    low = low_lanes((BLOCK, LANES))
    lane = lax.broadcasted_iota(jnp.int32, (ID_ROWS, LANES), 1)
    ids = jnp.zeros((ID_ROWS, LANES), jnp.int32)
    names.wait()
    for step in range(2):
        name = named[step, 2 * zh + zl]
        at = 2 * (4 * yh + zh) + step
        ids = jnp.where(lane == at, lax.shift_right_logical(name, 3), ids)
        ids = jnp.where(lane == at + RANDOMS, jnp.bitwise_and(name, 7), ids)
    ids = ids.astype(jnp.float32).astype(jnp.bfloat16)
    for rank in range(COLUMN):
        out_ref[rank, 2 * BLOCK :, :] = ids
    for row in range(2):
        copies[2 * row].wait()
        copies[2 * row + 1].wait()
        rows = slice(row * BLOCK, (row + 1) * BLOCK)
        for pair in range(COLUMN // 2):
            lanes = slice(pair * LANES, (pair + 1) * LANES)
            a = held[2 * row, :, lanes].astype(jnp.float32)
            b = held[2 * row + 1, :, lanes].astype(jnp.float32)
            a_turned = pltpu.roll(a, HEAD_DIM, 1)
            b_turned = pltpu.roll(b, HEAD_DIM, 1)
            out_ref[2 * pair, rows, :] = jnp.where(low, a, b_turned).astype(jnp.bfloat16)
            out_ref[2 * pair + 1, rows, :] = jnp.where(low, a_turned, b).astype(jnp.bfloat16)


def unpack_kernel(in_ref, o_ref, dq_ref, dk_ref, dv_ref):
    low = low_lanes((BLOCK, LANES))
    for row, (a_ref, b_ref) in enumerate(((dq_ref, o_ref), (dk_ref, dv_ref))):
        rows = slice(row * BLOCK, (row + 1) * BLOCK)
        for pair in range(COLUMN // 2):
            lanes = slice(pair * LANES, (pair + 1) * LANES)
            even = in_ref[2 * pair, rows, :].astype(jnp.float32)
            odd = in_ref[2 * pair + 1, rows, :].astype(jnp.float32)
            even_turned = pltpu.roll(even, HEAD_DIM, 1)
            odd_turned = pltpu.roll(odd, HEAD_DIM, 1)
            a_ref[:, lanes] = jnp.where(low, even, odd_turned).astype(jnp.bfloat16)
            b_ref[:, lanes] = jnp.where(low, even_turned, odd).astype(jnp.bfloat16)


def attend_kernel(own_ref, unit_ref, out_ref, grad_ref, own_grad_ref, shared, near, far):
    low = low_lanes((BLOCK, LANES))
    key_low = low_lanes((7 * BLOCK, LANES))
    far_keys = lax.broadcasted_iota(jnp.int32, (1, 7 * BLOCK), 1) // BLOCK == 2
    zero = jnp.zeros((BLOCK, LANES), jnp.bfloat16)
    x, yl, zl, core = (lax.axis_index(axis) for axis in ("x", "yl", "zl", "core"))
    column = 8 * x + 4 * yl + 2 * zl + core
    odd = zl == 1
    shared[...] = jnp.zeros(shared.shape, jnp.float32)

    def far_key(block):
        before = block - 1 + PARTNER if block % 4 > 0 else EDGE + block // 4
        after = block + 1 + PARTNER if block % 4 < 3 else EDGE + block // 4
        return jnp.where(odd, unit_ref[after], unit_ref[before])

    for start in range(0, COLUMN, GROUP):
        group = range(start, start + GROUP)
        rows, keys, both, stacked = {}, {}, {}, {}
        for block in group:
            pair = own_ref[block, :BLOCK, :]
            rows[block] = jnp.concatenate(
                [jnp.where(low, pair, zero), jnp.where(low, zero, pair)], axis=0
            )
            keys[block] = jnp.concatenate(
                [
                    own_ref[block, BLOCK : 2 * BLOCK, :],
                    unit_ref[PARTNER + block],
                    far_key(block),
                    unit_ref[2 * block],
                    unit_ref[2 * block + 1],
                    unit_ref[RANDOMS],
                    unit_ref[RANDOMS + 1],
                ],
                axis=0,
            )
            both[block] = lax.dot_general(
                rows[block],
                keys[block],
                (((1,), (1,)), ((), ())),
                preferred_element_type=jnp.float32,
            )
        for block in group:
            scores, prob_grad = both[block][:BLOCK], both[block][BLOCK:]
            if block == 0:
                scores = jnp.where(far_keys & (column == 0), -1e30, scores)
            if block == COLUMN - 1:
                scores = jnp.where(far_keys & (column == COLUMNS - 1), -1e30, scores)
            raised = jnp.exp2((scores - jnp.max(scores, axis=1, keepdims=True)) * EXP2_SCALE)
            probabilities = raised * (1.0 / jnp.sum(raised, axis=1, keepdims=True))
            probs_half = probabilities.astype(jnp.bfloat16)
            row_delta = jnp.sum(probs_half.astype(jnp.float32) * prob_grad, axis=1, keepdims=True)
            score_grad = (probabilities * (prob_grad - row_delta)).astype(jnp.bfloat16)
            stacked[block] = jnp.concatenate([score_grad, probs_half], axis=0)
        for block in group:
            mixed = jnp.dot(stacked[block], keys[block], preferred_element_type=jnp.float32)
            out_ref[block] = jnp.where(low, mixed[:BLOCK] * SCALE, mixed[BLOCK:]).astype(
                jnp.bfloat16
            )
            part = lax.dot_general(
                stacked[block],
                rows[block],
                (((0,), (0,)), ((), ())),
                preferred_element_type=jnp.float32,
            )
            part = jnp.where(key_low, part * SCALE, part)
            own_grad_ref[block] = part[:BLOCK]
            near[block] = part[BLOCK : 2 * BLOCK]
            far[block] = part[2 * BLOCK : 3 * BLOCK]
            for step in range(2):
                grad_ref[2 * block + step] = part[(3 + step) * BLOCK : (4 + step) * BLOCK].astype(
                    jnp.bfloat16
                )
                shared[step] += part[(5 + step) * BLOCK : (6 + step) * BLOCK]
    for step in range(2):
        grad_ref[RANDOMS + step] = shared[step].astype(jnp.bfloat16)
    none = jnp.zeros((BLOCK, LANES), jnp.float32)
    for block in range(COLUMN):
        after = far[block + 1] if block % 4 < 3 else none
        before = far[block - 1] if block % 4 > 0 else none
        grad_ref[PARTNER + block] = (near[block] + jnp.where(odd, before, after)).astype(
            jnp.bfloat16
        )
    for run in range(4):
        edge = jnp.where(odd, far[4 * run + 3], far[4 * run])
        grad_ref[EDGE + run] = edge.astype(jnp.bfloat16)
    for unit in range(USED, UNITS):
        grad_ref[unit] = zero


def swap(value, axis):
    return lax.all_to_all(value, axis, split_axis=0, concat_axis=0, tiled=True)


def body(query_rows, key_rows, value_rows, out_grad, random_blocks, global_blocks):
    half = jnp.bfloat16
    column, plane = ("yh", "zh"), ("x", "yl", "zl", "core")
    blocks = COLUMNS * COLUMN

    columns = np.arange(COLUMNS, dtype=np.int32)[:, None]
    places = np.arange(COLUMN, dtype=np.int32)[None]
    numbers = (
        columns // 8 * 128
        + columns // 4 % 2 * 16
        + columns % 2 * 8
        + columns // 2 % 2
        + places // 4 * 32
        + places % 4 * 2
    )
    odd_column = columns // 2 % 2
    partners = numbers + 1 - 2 * odd_column
    edges = np.where(odd_column == 1, numbers[:, 3::4] + 1, numbers[:, 0::4] - 1)

    hbm = pl.BlockSpec(memory_space=pltpu.HBM)
    vmem = pl.BlockSpec(memory_space=pltpu.VMEM)
    packed = vmem_call(
        pack_kernel,
        jax.ShapeDtypeStruct((COLUMN, 2 * BLOCK + ID_ROWS, LANES), half),
        [
            pltpu.VMEM((4, *query_rows.shape), half),
            pltpu.SMEM(random_blocks.shape[::-1], jnp.int32),
            pltpu.SemaphoreType.DMA((5,)),
        ],
        vmem=WHOLE_VMEM,
        in_specs=[hbm] * 5,
    )(random_blocks.T, query_rows, out_grad, key_rows, value_rows)
    own = swap(packed, column)

    spread = own[:, BLOCK : 2 * BLOCK].reshape(COLUMN, ROWS, COLUMNS, LANES).transpose(2, 1, 0, 3)
    spread = spread.reshape(COLUMNS, ROWS * COLUMN, LANES)
    named = jnp.sum(own[:, 2 * BLOCK :].astype(jnp.float32), axis=0).astype(half)
    named = jnp.broadcast_to(named[None], (COLUMNS, ID_ROWS, LANES))
    held = swap(jnp.concatenate([spread, named], axis=1), plane)

    held, global_blocks = lax.optimization_barrier((held, global_blocks))
    table = jnp.concatenate(
        [held[:, r * COLUMN : (r + 1) * COLUMN].reshape(blocks, LANES) for r in range(ROWS)], axis=1
    )
    ids = held[:, ROWS * COLUMN, : 2 * RANDOMS].astype(jnp.float32)
    ids = (ids[:, :RANDOMS] * 8 + ids[:, RANDOMS:]).astype(jnp.int32)
    shared = jnp.broadcast_to(global_blocks[None], (COLUMNS, 2))
    unused = np.full((COLUMNS, UNITS - USED), -1, np.int32)
    fixed = np.concatenate([partners, edges, unused], axis=1)
    ids = jnp.concatenate([ids, shared, fixed], axis=1).reshape(-1)
    numbers = numbers.reshape(-1)
    pick = (ids[:, None] == numbers[None, :]).astype(half)
    sent = jnp.dot(pick, table, preferred_element_type=jnp.float32).astype(half)
    units = swap(sent.reshape(COLUMNS, UNITS, ROWS * LANES), plane)
    units = units.reshape(COLUMNS, UNITS, ROWS, LANES).transpose(1, 2, 0, 3)
    units = units.reshape(UNITS, BLOCK, LANES)

    outs, unit_grad, own_grad = vmem_call(
        attend_kernel,
        (
            jax.ShapeDtypeStruct((COLUMN, BLOCK, LANES), half),
            jax.ShapeDtypeStruct((UNITS, BLOCK, LANES), half),
            jax.ShapeDtypeStruct((COLUMN, BLOCK, LANES), jnp.float32),
        ),
        [pltpu.VMEM((count, BLOCK, LANES), jnp.float32) for count in (2, COLUMN, COLUMN)],
        in_specs=[vmem, vmem],
    )(own, units)

    back = unit_grad.reshape(UNITS, ROWS, COLUMNS, LANES).transpose(2, 1, 0, 3)
    back = swap(back.reshape(COLUMNS, ROWS * UNITS, LANES), plane)
    ids, back = lax.optimization_barrier((ids, back))
    place = lax.optimization_barrier((numbers[:, None] == ids[None, :]).astype(half))
    total = [
        jnp.dot(
            place,
            back[:, r * UNITS : (r + 1) * UNITS].reshape(-1, LANES),
            preferred_element_type=jnp.float32,
        )
        .astype(half)
        .reshape(COLUMNS, COLUMN, LANES)
        for r in range(ROWS)
    ]
    total = swap(jnp.concatenate(total, axis=1), plane)
    total = total.reshape(COLUMNS, ROWS, COLUMN, LANES).transpose(2, 1, 0, 3)
    total = lax.optimization_barrier(total.reshape(COLUMN, BLOCK, LANES)).astype(jnp.float32)
    pair_grad = (own_grad + total).astype(half)
    result = swap(jnp.concatenate([outs, pair_grad], axis=1), column)
    return vmem_call(unpack_kernel, (jax.ShapeDtypeStruct(query_rows.shape, half),) * 4)(result)


def solution(mesh):
    split = Mesh(
        mesh.devices.reshape(4, 4, 2, 2, 4, 2), ("x", "yh", "yl", "core", "zh", "zl")
    )
    seq = ("x", "yh", "yl", "core")
    rows = P((*seq, "zh", "zl"), None)
    return jax.shard_map(
        body,
        mesh=split,
        in_specs=(rows, rows, rows, rows, P(seq, None), P()),
        out_specs=(rows, rows, rows, rows),
        check_vma=False,
    )
```

```python
import math

import jax
import jax.numpy as jnp
import numpy as np
from jax import lax
from jax.experimental import pallas as pl
from jax.experimental.pallas import tpu as pltpu
from jax.sharding import Mesh
from jax.sharding import PartitionSpec as P

HEAD_DIM = 64
BLOCK = 64
LANES = 128
COLUMN = 16
COLUMNS = 32
RANDOMS = 32
PARTNER = RANDOMS + 2
EDGE = PARTNER + COLUMN
USED = EDGE + 4
UNITS = 56
ROWS = 2
ID_ROWS = 8
GROUP = 8
SCALE = HEAD_DIM**-0.5
EXP2_SCALE = SCALE * math.log2(math.e)
VMEM = 48 * 1024 * 1024
WHOLE_VMEM = 60 * 1024 * 1024


def vmem_call(kernel, out_shape, scratch=(), vmem=VMEM, **specs):
    return pl.pallas_call(
        kernel,
        out_shape=out_shape,
        scratch_shapes=scratch,
        compiler_params=pltpu.CompilerParams(vmem_limit_bytes=vmem),
        **specs,
    )


def low_lanes(shape):
    return lax.broadcasted_iota(jnp.int32, shape, len(shape) - 1) < HEAD_DIM


def pack_kernel(random_ref, q_ref, g_ref, k_ref, v_ref, out_ref, held, named, arrived):
    names = pltpu.make_async_copy(random_ref, named, arrived.at[4])
    copies = [
        pltpu.make_async_copy(ref, held.at[i], arrived.at[i])
        for i, ref in enumerate((q_ref, g_ref, k_ref, v_ref))
    ]
    names.start()
    for copy in copies:
        copy.start()
    yh, zh, zl = (lax.axis_index(axis) for axis in ("yh", "zh", "zl"))
    low = low_lanes((BLOCK, LANES))
    lane = lax.broadcasted_iota(jnp.int32, (ID_ROWS, LANES), 1)
    ids = jnp.zeros((ID_ROWS, LANES), jnp.int32)
    names.wait()
    for step in range(2):
        name = named[step, 2 * zh + zl]
        at = 2 * (4 * yh + zh) + step
        ids = jnp.where(lane == at, lax.shift_right_logical(name, 3), ids)
        ids = jnp.where(lane == at + RANDOMS, jnp.bitwise_and(name, 7), ids)
    ids = ids.astype(jnp.float32).astype(jnp.bfloat16)
    for rank in range(COLUMN):
        out_ref[rank, 2 * BLOCK :, :] = ids
    for row in range(2):
        copies[2 * row].wait()
        copies[2 * row + 1].wait()
        rows = slice(row * BLOCK, (row + 1) * BLOCK)
        for pair in range(COLUMN // 2):
            lanes = slice(pair * LANES, (pair + 1) * LANES)
            a = held[2 * row, :, lanes].astype(jnp.float32)
            b = held[2 * row + 1, :, lanes].astype(jnp.float32)
            a_turned = pltpu.roll(a, HEAD_DIM, 1)
            b_turned = pltpu.roll(b, HEAD_DIM, 1)
            out_ref[2 * pair, rows, :] = jnp.where(low, a, b_turned).astype(jnp.bfloat16)
            out_ref[2 * pair + 1, rows, :] = jnp.where(low, a_turned, b).astype(jnp.bfloat16)


def unpack_kernel(in_ref, o_ref, dq_ref, dk_ref, dv_ref):
    low = low_lanes((BLOCK, LANES))
    for row, (a_ref, b_ref) in enumerate(((dq_ref, o_ref), (dk_ref, dv_ref))):
        rows = slice(row * BLOCK, (row + 1) * BLOCK)
        for pair in range(COLUMN // 2):
            lanes = slice(pair * LANES, (pair + 1) * LANES)
            even = in_ref[2 * pair, rows, :].astype(jnp.float32)
            odd = in_ref[2 * pair + 1, rows, :].astype(jnp.float32)
            even_turned = pltpu.roll(even, HEAD_DIM, 1)
            odd_turned = pltpu.roll(odd, HEAD_DIM, 1)
            a_ref[:, lanes] = jnp.where(low, even, odd_turned).astype(jnp.bfloat16)
            b_ref[:, lanes] = jnp.where(low, even_turned, odd).astype(jnp.bfloat16)


def attend_kernel(own_ref, unit_ref, out_ref, grad_ref, own_grad_ref, shared, near, far):
    low = low_lanes((BLOCK, LANES))
    key_low = low_lanes((7 * BLOCK, LANES))
    far_keys = lax.broadcasted_iota(jnp.int32, (1, 7 * BLOCK), 1) // BLOCK == 2
    zero = jnp.zeros((BLOCK, LANES), jnp.bfloat16)
    x, yl, zl, core = (lax.axis_index(axis) for axis in ("x", "yl", "zl", "core"))
    column = 16 * zl + 8 * yl + 2 * x + core
    odd = zl == 1
    shared[...] = jnp.zeros(shared.shape, jnp.float32)

    def far_key(block):
        before = block - 1 + PARTNER if block % 4 > 0 else EDGE + block // 4
        after = block + 1 + PARTNER if block % 4 < 3 else EDGE + block // 4
        return jnp.where(odd, unit_ref[after], unit_ref[before])

    for start in range(0, COLUMN, GROUP):
        group = range(start, start + GROUP)
        rows, keys, both, stacked = {}, {}, {}, {}
        for block in group:
            pair = own_ref[block, :BLOCK, :]
            rows[block] = jnp.concatenate(
                [jnp.where(low, pair, zero), jnp.where(low, zero, pair)], axis=0
            )
            keys[block] = jnp.concatenate(
                [
                    own_ref[block, BLOCK : 2 * BLOCK, :],
                    unit_ref[PARTNER + block],
                    far_key(block),
                    unit_ref[2 * block],
                    unit_ref[2 * block + 1],
                    unit_ref[RANDOMS],
                    unit_ref[RANDOMS + 1],
                ],
                axis=0,
            )
            both[block] = lax.dot_general(
                rows[block],
                keys[block],
                (((1,), (1,)), ((), ())),
                preferred_element_type=jnp.float32,
            )
        for block in group:
            scores, prob_grad = both[block][:BLOCK], both[block][BLOCK:]
            if block == 0:
                scores = jnp.where(far_keys & (column == 0), -1e30, scores)
            if block == COLUMN - 1:
                scores = jnp.where(far_keys & (column == COLUMNS - 1), -1e30, scores)
            raised = jnp.exp2((scores - jnp.max(scores, axis=1, keepdims=True)) * EXP2_SCALE)
            probabilities = raised * (1.0 / jnp.sum(raised, axis=1, keepdims=True))
            probs_half = probabilities.astype(jnp.bfloat16)
            row_delta = jnp.sum(probs_half.astype(jnp.float32) * prob_grad, axis=1, keepdims=True)
            score_grad = (probabilities * (prob_grad - row_delta)).astype(jnp.bfloat16)
            stacked[block] = jnp.concatenate([score_grad, probs_half], axis=0)
        for block in group:
            mixed = jnp.dot(stacked[block], keys[block], preferred_element_type=jnp.float32)
            out_ref[block] = jnp.where(low, mixed[:BLOCK] * SCALE, mixed[BLOCK:]).astype(
                jnp.bfloat16
            )
            part = lax.dot_general(
                stacked[block],
                rows[block],
                (((0,), (0,)), ((), ())),
                preferred_element_type=jnp.float32,
            )
            part = jnp.where(key_low, part * SCALE, part)
            own_grad_ref[block] = part[:BLOCK]
            near[block] = part[BLOCK : 2 * BLOCK]
            far[block] = part[2 * BLOCK : 3 * BLOCK]
            for step in range(2):
                grad_ref[2 * block + step] = part[(3 + step) * BLOCK : (4 + step) * BLOCK].astype(
                    jnp.bfloat16
                )
                shared[step] += part[(5 + step) * BLOCK : (6 + step) * BLOCK]
    for step in range(2):
        grad_ref[RANDOMS + step] = shared[step].astype(jnp.bfloat16)
    none = jnp.zeros((BLOCK, LANES), jnp.float32)
    for block in range(COLUMN):
        after = far[block + 1] if block % 4 < 3 else none
        before = far[block - 1] if block % 4 > 0 else none
        grad_ref[PARTNER + block] = (near[block] + jnp.where(odd, before, after)).astype(
            jnp.bfloat16
        )
    for run in range(4):
        edge = jnp.where(odd, far[4 * run + 3], far[4 * run])
        grad_ref[EDGE + run] = edge.astype(jnp.bfloat16)
    for unit in range(USED, UNITS):
        grad_ref[unit] = zero


def swap(value, axis):
    return lax.all_to_all(value, axis, split_axis=0, concat_axis=0, tiled=True)


def body(query_rows, key_rows, value_rows, out_grad, random_blocks, global_blocks):
    half = jnp.bfloat16
    column, plane = ("yh", "zh"), ("zl", "yl", "x", "core")
    blocks = COLUMNS * COLUMN

    columns = np.arange(COLUMNS, dtype=np.int32)[:, None]
    places = np.arange(COLUMN, dtype=np.int32)[None]
    numbers = (
        columns // 2 % 4 * 128
        + columns // 8 % 2 * 16
        + columns % 2 * 8
        + columns // 16
        + places // 4 * 32
        + places % 4 * 2
    )
    odd_column = columns // 16
    partners = numbers + 1 - 2 * odd_column
    edges = np.where(odd_column == 1, numbers[:, 3::4] + 1, numbers[:, 0::4] - 1)

    hbm = pl.BlockSpec(memory_space=pltpu.HBM)
    vmem = pl.BlockSpec(memory_space=pltpu.VMEM)
    packed = vmem_call(
        pack_kernel,
        jax.ShapeDtypeStruct((COLUMN, 2 * BLOCK + ID_ROWS, LANES), half),
        [
            pltpu.VMEM((4, *query_rows.shape), half),
            pltpu.SMEM(random_blocks.shape[::-1], jnp.int32),
            pltpu.SemaphoreType.DMA((5,)),
        ],
        vmem=WHOLE_VMEM,
        in_specs=[hbm] * 5,
    )(random_blocks.T, query_rows, out_grad, key_rows, value_rows)
    own = swap(packed, column)

    spread = own[:, BLOCK : 2 * BLOCK].reshape(COLUMN, ROWS, COLUMNS, LANES).transpose(2, 1, 0, 3)
    spread = spread.reshape(COLUMNS, ROWS * COLUMN, LANES)
    named = jnp.sum(own[:, 2 * BLOCK :].astype(jnp.float32), axis=0).astype(half)
    named = jnp.broadcast_to(named[None], (COLUMNS, ID_ROWS, LANES))
    held = swap(jnp.concatenate([spread, named], axis=1), plane)

    held, global_blocks = lax.optimization_barrier((held, global_blocks))
    table = jnp.concatenate(
        [held[:, r * COLUMN : (r + 1) * COLUMN].reshape(blocks, LANES) for r in range(ROWS)], axis=1
    )
    ids = held[:, ROWS * COLUMN, : 2 * RANDOMS].astype(jnp.float32)
    ids = (ids[:, :RANDOMS] * 8 + ids[:, RANDOMS:]).astype(jnp.int32)
    shared = jnp.broadcast_to(global_blocks[None], (COLUMNS, 2))
    unused = np.full((COLUMNS, UNITS - USED), -1, np.int32)
    fixed = np.concatenate([partners, edges, unused], axis=1)
    ids = jnp.concatenate([ids, shared, fixed], axis=1).reshape(-1)
    numbers = numbers.reshape(-1)
    pick = (ids[:, None] == numbers[None, :]).astype(half)
    sent = jnp.dot(pick, table, preferred_element_type=jnp.float32).astype(half)
    units = swap(sent.reshape(COLUMNS, UNITS, ROWS * LANES), plane)
    units = units.reshape(COLUMNS, UNITS, ROWS, LANES).transpose(1, 2, 0, 3)
    units = units.reshape(UNITS, BLOCK, LANES)

    outs, unit_grad, own_grad = vmem_call(
        attend_kernel,
        (
            jax.ShapeDtypeStruct((COLUMN, BLOCK, LANES), half),
            jax.ShapeDtypeStruct((UNITS, BLOCK, LANES), half),
            jax.ShapeDtypeStruct((COLUMN, BLOCK, LANES), jnp.float32),
        ),
        [pltpu.VMEM((count, BLOCK, LANES), jnp.float32) for count in (2, COLUMN, COLUMN)],
        in_specs=[vmem, vmem],
    )(own, units)

    back = unit_grad.reshape(UNITS, ROWS, COLUMNS, LANES).transpose(2, 1, 0, 3)
    back = swap(back.reshape(COLUMNS, ROWS * UNITS, LANES), plane)
    place = (numbers[:, None] == ids[None, :]).astype(half)
    total = [
        jnp.dot(
            place,
            back[:, r * UNITS : (r + 1) * UNITS].reshape(-1, LANES),
            preferred_element_type=jnp.float32,
        )
        .astype(half)
        .reshape(COLUMNS, COLUMN, LANES)
        for r in range(ROWS)
    ]
    total = swap(jnp.concatenate(total, axis=1), plane)
    total = total.reshape(COLUMNS, ROWS, COLUMN, LANES).transpose(2, 1, 0, 3)
    total = total.reshape(COLUMN, BLOCK, LANES).astype(jnp.float32)
    pair_grad = (own_grad + total).astype(half)
    result = swap(jnp.concatenate([outs, pair_grad], axis=1), column)
    return vmem_call(unpack_kernel, (jax.ShapeDtypeStruct(query_rows.shape, half),) * 4)(result)


def solution(mesh):
    split = Mesh(
        mesh.devices.reshape(4, 4, 2, 2, 4, 2), ("x", "yh", "yl", "core", "zh", "zl")
    )
    seq = ("x", "yh", "yl", "core")
    rows = P((*seq, "zh", "zl"), None)
    return jax.shard_map(
        body,
        mesh=split,
        in_specs=(rows, rows, rows, rows, P(seq, None), P()),
        out_specs=(rows, rows, rows, rows),
        check_vma=False,
    )
```

```python
import math

import jax
import jax.numpy as jnp
import numpy as np
from jax import lax
from jax.experimental import pallas as pl
from jax.experimental.pallas import tpu as pltpu
from jax.sharding import Mesh
from jax.sharding import PartitionSpec as P

HEAD_DIM = 64
BLOCK = 64
LANES = 128
COLUMN = 16
COLUMNS = 32
RANDOMS = 32
PARTNER = RANDOMS + 2
EDGE = PARTNER + COLUMN
USED = EDGE + 4
UNITS = 56
ROWS = 2
ID_ROWS = 8
GROUP = 8
SCALE = HEAD_DIM**-0.5
EXP2_SCALE = SCALE * math.log2(math.e)
VMEM = 48 * 1024 * 1024
WHOLE_VMEM = 60 * 1024 * 1024


def vmem_call(kernel, out_shape, scratch=(), vmem=VMEM, **specs):
    return pl.pallas_call(
        kernel,
        out_shape=out_shape,
        scratch_shapes=scratch,
        compiler_params=pltpu.CompilerParams(vmem_limit_bytes=vmem),
        **specs,
    )


def low_lanes(shape):
    return lax.broadcasted_iota(jnp.int32, shape, len(shape) - 1) < HEAD_DIM


def pack_kernel(random_ref, q_ref, g_ref, k_ref, v_ref, out_ref, held, named, arrived):
    names = pltpu.make_async_copy(random_ref, named, arrived.at[4])
    copies = [
        pltpu.make_async_copy(ref, held.at[i], arrived.at[i])
        for i, ref in enumerate((q_ref, g_ref, k_ref, v_ref))
    ]
    names.start()
    for copy in copies:
        copy.start()
    yh, zh, zl = (lax.axis_index(axis) for axis in ("yh", "zh", "zl"))
    low = low_lanes((BLOCK, LANES))
    lane = lax.broadcasted_iota(jnp.int32, (ID_ROWS, LANES), 1)
    ids = jnp.zeros((ID_ROWS, LANES), jnp.int32)
    names.wait()
    for step in range(2):
        name = named[step, 2 * zh + zl]
        at = 2 * (4 * yh + zh) + step
        ids = jnp.where(lane == at, lax.shift_right_logical(name, 3), ids)
        ids = jnp.where(lane == at + RANDOMS, jnp.bitwise_and(name, 7), ids)
    ids = ids.astype(jnp.float32).astype(jnp.bfloat16)
    for rank in range(COLUMN):
        out_ref[rank, 2 * BLOCK :, :] = ids
    for row in range(2):
        copies[2 * row].wait()
        copies[2 * row + 1].wait()
        rows = slice(row * BLOCK, (row + 1) * BLOCK)
        for pair in range(COLUMN // 2):
            lanes = slice(pair * LANES, (pair + 1) * LANES)
            a = held[2 * row, :, lanes].astype(jnp.float32)
            b = held[2 * row + 1, :, lanes].astype(jnp.float32)
            a_turned = pltpu.roll(a, HEAD_DIM, 1)
            b_turned = pltpu.roll(b, HEAD_DIM, 1)
            out_ref[2 * pair, rows, :] = jnp.where(low, a, b_turned).astype(jnp.bfloat16)
            out_ref[2 * pair + 1, rows, :] = jnp.where(low, a_turned, b).astype(jnp.bfloat16)


def unpack_kernel(in_ref, o_ref, dq_ref, dk_ref, dv_ref):
    low = low_lanes((BLOCK, LANES))
    for row, (a_ref, b_ref) in enumerate(((dq_ref, o_ref), (dk_ref, dv_ref))):
        rows = slice(row * BLOCK, (row + 1) * BLOCK)
        for pair in range(COLUMN // 2):
            lanes = slice(pair * LANES, (pair + 1) * LANES)
            even = in_ref[2 * pair, rows, :].astype(jnp.float32)
            odd = in_ref[2 * pair + 1, rows, :].astype(jnp.float32)
            even_turned = pltpu.roll(even, HEAD_DIM, 1)
            odd_turned = pltpu.roll(odd, HEAD_DIM, 1)
            a_ref[:, lanes] = jnp.where(low, even, odd_turned).astype(jnp.bfloat16)
            b_ref[:, lanes] = jnp.where(low, even_turned, odd).astype(jnp.bfloat16)


def attend_kernel(own_ref, unit_ref, out_ref, grad_ref, own_grad_ref, shared, near, far):
    low = low_lanes((BLOCK, LANES))
    key_low = low_lanes((7 * BLOCK, LANES))
    far_keys = lax.broadcasted_iota(jnp.int32, (1, 7 * BLOCK), 1) // BLOCK == 2
    zero = jnp.zeros((BLOCK, LANES), jnp.bfloat16)
    x, yl, zl, core = (lax.axis_index(axis) for axis in ("x", "yl", "zl", "core"))
    column = 8 * x + 4 * yl + 2 * zl + core
    odd = zl == 1
    shared[...] = jnp.zeros(shared.shape, jnp.float32)

    def far_key(block):
        before = block - 1 + PARTNER if block % 4 > 0 else EDGE + block // 4
        after = block + 1 + PARTNER if block % 4 < 3 else EDGE + block // 4
        return jnp.where(odd, unit_ref[after], unit_ref[before])

    for start in range(0, COLUMN, GROUP):
        group = range(start, start + GROUP)
        rows, keys, both, stacked = {}, {}, {}, {}
        for block in group:
            pair = own_ref[block, :BLOCK, :]
            rows[block] = jnp.concatenate(
                [jnp.where(low, pair, zero), jnp.where(low, zero, pair)], axis=0
            )
            keys[block] = jnp.concatenate(
                [
                    own_ref[block, BLOCK : 2 * BLOCK, :],
                    unit_ref[PARTNER + block],
                    far_key(block),
                    unit_ref[2 * block],
                    unit_ref[2 * block + 1],
                    unit_ref[RANDOMS],
                    unit_ref[RANDOMS + 1],
                ],
                axis=0,
            )
            both[block] = lax.dot_general(
                rows[block],
                keys[block],
                (((1,), (1,)), ((), ())),
                preferred_element_type=jnp.float32,
            )
        for block in group:
            scores, prob_grad = both[block][:BLOCK], both[block][BLOCK:]
            if block == 0:
                scores = jnp.where(far_keys & (column == 0), -1e30, scores)
            if block == COLUMN - 1:
                scores = jnp.where(far_keys & (column == COLUMNS - 1), -1e30, scores)
            raised = jnp.exp2((scores - jnp.max(scores, axis=1, keepdims=True)) * EXP2_SCALE)
            probabilities = raised * (1.0 / jnp.sum(raised, axis=1, keepdims=True))
            probs_half = probabilities.astype(jnp.bfloat16)
            row_delta = jnp.sum(probs_half.astype(jnp.float32) * prob_grad, axis=1, keepdims=True)
            score_grad = (probabilities * (prob_grad - row_delta)).astype(jnp.bfloat16)
            stacked[block] = jnp.concatenate([score_grad, probs_half], axis=0)
        for block in group:
            mixed = jnp.dot(stacked[block], keys[block], preferred_element_type=jnp.float32)
            out_ref[block] = jnp.where(low, mixed[:BLOCK] * SCALE, mixed[BLOCK:]).astype(
                jnp.bfloat16
            )
            part = lax.dot_general(
                stacked[block],
                rows[block],
                (((0,), (0,)), ((), ())),
                preferred_element_type=jnp.float32,
            )
            part = jnp.where(key_low, part * SCALE, part)
            own_grad_ref[block] = part[:BLOCK]
            near[block] = part[BLOCK : 2 * BLOCK]
            far[block] = part[2 * BLOCK : 3 * BLOCK]
            for step in range(2):
                grad_ref[2 * block + step] = part[(3 + step) * BLOCK : (4 + step) * BLOCK].astype(
                    jnp.bfloat16
                )
                shared[step] += part[(5 + step) * BLOCK : (6 + step) * BLOCK]
    for step in range(2):
        grad_ref[RANDOMS + step] = shared[step].astype(jnp.bfloat16)
    none = jnp.zeros((BLOCK, LANES), jnp.float32)
    for block in range(COLUMN):
        after = far[block + 1] if block % 4 < 3 else none
        before = far[block - 1] if block % 4 > 0 else none
        grad_ref[PARTNER + block] = (near[block] + jnp.where(odd, before, after)).astype(
            jnp.bfloat16
        )
    for run in range(4):
        edge = jnp.where(odd, far[4 * run + 3], far[4 * run])
        grad_ref[EDGE + run] = edge.astype(jnp.bfloat16)
    for unit in range(USED, UNITS):
        grad_ref[unit] = zero


def swap(value, axis):
    return lax.all_to_all(value, axis, split_axis=0, concat_axis=0, tiled=True)


def body(query_rows, key_rows, value_rows, out_grad, random_blocks, global_blocks):
    half = jnp.bfloat16
    column, plane = ("yh", "zh"), ("x", "yl", "zl", "core")
    blocks = COLUMNS * COLUMN

    columns = np.arange(COLUMNS, dtype=np.int32)[:, None]
    places = np.arange(COLUMN, dtype=np.int32)[None]
    numbers = (
        columns // 8 * 128
        + columns // 4 % 2 * 16
        + columns % 2 * 8
        + columns // 2 % 2
        + places // 4 * 32
        + places % 4 * 2
    )
    odd_column = columns // 2 % 2
    partners = numbers + 1 - 2 * odd_column
    edges = np.where(odd_column == 1, numbers[:, 3::4] + 1, numbers[:, 0::4] - 1)

    hbm = pl.BlockSpec(memory_space=pltpu.HBM)
    vmem = pl.BlockSpec(memory_space=pltpu.VMEM)
    packed = vmem_call(
        pack_kernel,
        jax.ShapeDtypeStruct((COLUMN, 2 * BLOCK + ID_ROWS, LANES), half),
        [
            pltpu.VMEM((4, *query_rows.shape), half),
            pltpu.SMEM(random_blocks.shape[::-1], jnp.int32),
            pltpu.SemaphoreType.DMA((5,)),
        ],
        vmem=WHOLE_VMEM,
        in_specs=[hbm] * 5,
    )(random_blocks.T, query_rows, out_grad, key_rows, value_rows)
    own = swap(packed, column)

    spread = own[:, BLOCK : 2 * BLOCK].reshape(COLUMN, ROWS, COLUMNS, LANES).transpose(2, 1, 0, 3)
    spread = spread.reshape(COLUMNS, ROWS * COLUMN, LANES)
    named = jnp.sum(own[:, 2 * BLOCK :].astype(jnp.float32), axis=0).astype(half)
    named = jnp.broadcast_to(named[None], (COLUMNS, ID_ROWS, LANES))
    held = swap(jnp.concatenate([spread, named], axis=1), plane)

    held, global_blocks = lax.optimization_barrier((held, global_blocks))
    table = jnp.concatenate(
        [held[:, r * COLUMN : (r + 1) * COLUMN].reshape(blocks, LANES) for r in range(ROWS)], axis=1
    )
    ids = held[:, ROWS * COLUMN, : 2 * RANDOMS].astype(jnp.float32)
    ids = (ids[:, :RANDOMS] * 8 + ids[:, RANDOMS:]).astype(jnp.int32)
    shared = jnp.broadcast_to(global_blocks[None], (COLUMNS, 2))
    unused = np.full((COLUMNS, UNITS - USED), -1, np.int32)
    fixed = np.concatenate([partners, edges, unused], axis=1)
    ids = jnp.concatenate([ids, shared, fixed], axis=1).reshape(-1)
    numbers = numbers.reshape(-1)
    pick = (ids[:, None] == numbers[None, :]).astype(half)
    sent = jnp.dot(pick, table, preferred_element_type=jnp.float32).astype(half)
    units = swap(sent.reshape(COLUMNS, UNITS, ROWS * LANES), plane)
    units = units.reshape(COLUMNS, UNITS, ROWS, LANES).transpose(1, 2, 0, 3)
    units = units.reshape(UNITS, BLOCK, LANES)

    outs, unit_grad, own_grad = vmem_call(
        attend_kernel,
        (
            jax.ShapeDtypeStruct((COLUMN, BLOCK, LANES), half),
            jax.ShapeDtypeStruct((UNITS, BLOCK, LANES), half),
            jax.ShapeDtypeStruct((COLUMN, BLOCK, LANES), jnp.float32),
        ),
        [pltpu.VMEM((count, BLOCK, LANES), jnp.float32) for count in (2, COLUMN, COLUMN)],
        in_specs=[vmem, vmem],
    )(own, units)

    back = unit_grad.reshape(UNITS, ROWS, COLUMNS, LANES).transpose(2, 1, 0, 3)
    back = swap(back.reshape(COLUMNS, ROWS * UNITS, LANES), plane)
    place = (numbers[:, None] == ids[None, :]).astype(half)
    total = [
        jnp.dot(
            place,
            back[:, r * UNITS : (r + 1) * UNITS].reshape(-1, LANES),
            preferred_element_type=jnp.float32,
        )
        .astype(half)
        .reshape(COLUMNS, COLUMN, LANES)
        for r in range(ROWS)
    ]
    total = swap(jnp.concatenate(total, axis=1), plane)
    total = total.reshape(COLUMNS, ROWS, COLUMN, LANES).transpose(2, 1, 0, 3)
    total = lax.optimization_barrier(total.reshape(COLUMN, BLOCK, LANES)).astype(jnp.float32)
    pair_grad = (own_grad + total).astype(half)
    result = swap(jnp.concatenate([outs, pair_grad], axis=1), column)
    return vmem_call(unpack_kernel, (jax.ShapeDtypeStruct(query_rows.shape, half),) * 4)(result)


def solution(mesh):
    split = Mesh(
        mesh.devices.reshape(4, 4, 2, 2, 4, 2), ("x", "yh", "yl", "core", "zh", "zl")
    )
    seq = ("x", "yh", "yl", "core")
    rows = P((*seq, "zh", "zl"), None)
    return jax.shard_map(
        body,
        mesh=split,
        in_specs=(rows, rows, rows, rows, P(seq, None), P()),
        out_specs=(rows, rows, rows, rows),
        check_vma=False,
    )
```
